128 devices in a mesh: dom: 128 (over x, y, z, core).
Axes of the slice: x: 4, y: 4, z: 4, core: 2. Of those that a mesh axis runs over, the one named last changes fastest.
Arguments:
- density: float32 [1048576], P('dom'), may hold values from 0 to 1
- gradient: float32 [3, 1048576], P(None, 'dom'), may hold values from -3 to 3
- elem_size: float32 [1048576], P('dom'), may hold values from 0.5 to 2
- history: float32 [2, 1048576], P(None, 'dom'), may hold values from -6 to 6
- refine_flags: int32 [1048576], P('dom'), may hold values 0 or 1
- face_neighbor: int32 [6, 1048576], P(None, 'dom'), may hold values from 0 to 12287
- face_weight: float32 [6, 1048576], P(None, 'dom'), may hold values from 0.05 to 0.5
- ghost_send: int32 [512, 1024], P('dom'), may hold values from 0 to 8191
- new_counts: int32 [128], replicated, may hold values from 7168 to 9216, as said below
Outputs:
- indicator: float32 [1048576], P('dom')
- child_fields: float32 [3, 8, 1179648], P(None, None, 'dom')
The draws below stay inside these ranges and needn't reach their ends.
Inputs may be any that keep to these rules, and one draw needn't show every extreme that they name: `new_counts`: the new partition boundaries b_q lie within 512 elements of q * 8192, so every element moves at most one partition along the curve; some boundary moves by exactly 512 in each direction, and some partition gets 9216 elements.
All inputs are finite; a program needn't handle non-finite values. No bound on the sum of `refine_flags` on one device may be relied on, other than what follows from the above.
Results may differ from the reference program's by a relative error of at most 0.00002.
Values sent between devices are 32-bit elements; how exact they have to be, the bound alone decides.
A program may use at most 128 MiB of HBM per device.

```python
import math
import jax
import jax.numpy as jnp

E_DEV = 8192
GH = 1024
TOTAL = 1048576
PEER = 512
CAP_IN = 9216
HOP = 16
N_DOM = 128


def draw_new_counts(key, part):
    key = jax.random.fold_in(key, 11)
    moves = jax.random.randint(key, (N_DOM + 1,), -PEER, PEER + 1).astype(jnp.int32)
    moves = moves.at[0].set(0).at[N_DOM].set(0)
    moves = moves.at[1].set(PEER).at[2].set(-PEER).at[3].set(-PEER).at[4].set(PEER)
    return (E_DEV + moves[1:] - moves[:-1]).astype(jnp.int32)


def place_ends(values, key, smallest, high):
    extent = values.shape
    spot = [jax.random.randint(jax.random.fold_in(key, axis), (), 0, extent[axis]) for axis in range(len(extent))]
    values = values.at[tuple(spot)].set(smallest)
    longest = extent.index(max(extent))
    spot[longest] = (spot[longest] + 1) % extent[longest]
    return values.at[tuple(spot)].set(high)


def levels(rng, shape, pieces, least, top_value):
    level = 1.0
    for axis_at, shards_of in pieces:
        steps = jax.random.uniform(jax.random.fold_in(jax.random.fold_in(rng, 6), axis_at), (shards_of,), jnp.float32, least / len(pieces), top_value / len(pieces))
        level = level * jnp.repeat(jnp.exp(steps), shape[axis_at] // shards_of).reshape((-1,) + (1,) * (len(shape) - 1 - axis_at))
    return level


def gaussian(rng, shape, deviation, reach, cuts=(), held_as=jnp.bfloat16):
    gain = levels(rng, shape, cuts, -0.22, 0.18) if cuts else 1.0
    drawn = jax.random.normal(rng, shape, jnp.float32) * deviation * gain
    return jnp.minimum(jnp.maximum(drawn, -reach), reach).astype(held_as)


def setup_inputs(seed: int = 0) -> dict:
    arg_keys = jax.random.split(jax.random.key(seed), 10)
    density = jnp.clip(1.0 * jax.random.uniform(arg_keys[0], (TOTAL,), jnp.float32) ** levels(arg_keys[0], (TOTAL,), ((0, 128),), -0.2, 0.2), 0.0, 1.0)
    gradient = gaussian(arg_keys[1], (3, TOTAL), 0.4, 3.0, ((1, 128),), jnp.float32)
    elem_size = jnp.clip(jnp.exp(math.log(2.0) - 1.3862944 * jax.random.uniform(arg_keys[2], (TOTAL,), jnp.float32) ** levels(arg_keys[2], (TOTAL,), ((0, 128),), -0.2, 0.2)), 0.5, 2.0)
    history = gaussian(arg_keys[3], (2, TOTAL), 1.0, 6.0, ((1, 128),), jnp.float32)
    refine_flags = place_ends((jax.random.randint(arg_keys[4], (TOTAL,), 0, 2) < 1).astype(jnp.int32), jax.random.fold_in(arg_keys[4], 1), 0, 1)
    face_neighbor = place_ends(jax.random.randint(arg_keys[5], (6, TOTAL), 0, E_DEV + 4 * GH), jax.random.fold_in(arg_keys[5], 1), 0, (E_DEV + 4 * GH) - 1).astype(jnp.int32)
    face_weight = jnp.clip(jnp.exp(math.log(0.5) - 2.3025851 * jax.random.uniform(arg_keys[6], (6, TOTAL), jnp.float32) ** levels(arg_keys[6], (6, TOTAL), ((1, 128),), -0.2, 0.2)), 0.05, 0.5)
    ghost_send = place_ends(jax.random.randint(arg_keys[7], (4 * N_DOM, GH), 0, E_DEV), jax.random.fold_in(arg_keys[7], 1), 0, E_DEV - 1).astype(jnp.int32)
    new_counts = draw_new_counts(jax.random.fold_in(arg_keys[9], 71), 0)
    return {"density": density, "gradient": gradient, "elem_size": elem_size, "history": history, "refine_flags": refine_flags, "face_neighbor": face_neighbor, "face_weight": face_weight, "ghost_send": ghost_send, "new_counts": new_counts}


def prolong(density, gradient, elem_size, history, flags):
    child_ids = jnp.arange(8, dtype=jnp.int32)
    sign_x = (2 * (child_ids % 2) - 1).astype(jnp.float32)[:, None]
    sign_y = (2 * ((child_ids // 2) % 2) - 1).astype(jnp.float32)[:, None]
    sign_z = (2 * ((child_ids // 4) % 2) - 1).astype(jnp.float32)[:, None]
    slope = sign_x * gradient[0][None, :] + sign_y * gradient[1][None, :] + sign_z * gradient[2][None, :]
    shifted = density[None, :] + 0.25 * elem_size[None, :] * slope
    refined = (flags > 0)[None, :]
    first_child = (child_ids == 0)[:, None]
    kept_mask = jnp.logical_or(refined, first_child)
    zero_val = jnp.zeros((), jnp.float32)
    density_kids = jnp.where(refined, shifted, jnp.where(first_child, density[None, :], zero_val))
    older = jnp.where(kept_mask, history[0][None, :], zero_val)
    oldest = jnp.where(kept_mask, history[1][None, :], zero_val)
    return jnp.stack([density_kids, older, oldest])


def face_jumps(extended, neighbors, weights, elements):
    across = jnp.take(extended, neighbors.reshape(-1), axis=1).reshape(3, 6, elements)
    own = extended[:, :elements]
    jump = own[:, None, :] - across
    squares = jump[0] * jump[0] + jump[1] * jump[1] + jump[2] * jump[2]
    return jnp.sum(weights * squares, axis=0)


def reference(density, gradient, elem_size, history, refine_flags, face_neighbor, face_weight, ghost_send, new_counts):
    members = N_DOM
    elements = E_DEV
    offsets = jnp.array([1, -1, HOP, -HOP], jnp.int32)
    device_ids = jnp.arange(members, dtype=jnp.int32)
    sources = (device_ids[:, None] - offsets[None, :]) % members
    picked = jnp.take(ghost_send, (sources * 4 + jnp.arange(4, dtype=jnp.int32)[None, :]).reshape(-1), axis=0)
    picked = picked.reshape(members, 4, GH)
    curve_pos = (sources[:, :, None] * elements + picked).astype(jnp.int32)
    ghost_vals = jnp.take(gradient, curve_pos.reshape(-1), axis=1).reshape(3, members, 4, GH)
    ghost_vals = jnp.transpose(ghost_vals, (1, 0, 2, 3)).reshape(members, 3, 4 * GH)
    grad_blocks = jnp.transpose(gradient.reshape(3, members, elements), (1, 0, 2))
    extended = jnp.concatenate([grad_blocks, ghost_vals], axis=2)
    nbr_all = jnp.transpose(face_neighbor.reshape(6, members, elements), (1, 0, 2))
    weight_all = jnp.transpose(face_weight.reshape(6, members, elements), (1, 0, 2))

    def one_part(extended_p, nbr_p, weight_p):
        return face_jumps(extended_p, nbr_p, weight_p, elements)

    indicator = jax.vmap(one_part)(extended, nbr_all, weight_all).reshape(-1)
    boundaries = jnp.concatenate([jnp.zeros((1,), jnp.int32), jnp.cumsum(new_counts).astype(jnp.int32)])
    position = jnp.arange(TOTAL, dtype=jnp.int32)
    new_owner = jnp.searchsorted(boundaries[1:], position, side="right").astype(jnp.int32)
    new_slot = (new_owner * CAP_IN + position - jnp.take(boundaries, new_owner)).astype(jnp.int32)
    children = prolong(density, gradient, elem_size, history, refine_flags)
    child_fields = jnp.zeros((3, 8, members * CAP_IN), jnp.float32).at[:, :, new_slot].set(children)
    return indicator, child_fields
```

```python
import functools

import jax
import jax.numpy as jnp
from jax import lax
from jax.experimental import pallas as pl
from jax.experimental.pallas import tpu as pltpu
from jax.sharding import PartitionSpec as P

ELEMENTS = 8192
ROWS = ELEMENTS // 128
BLOCKS = ROWS // 8
GHOST = 1024
MARGIN = 512
MARGIN_ROWS = MARGIN // 128
CAPACITY = ELEMENTS + 2 * MARGIN
OUT_ROWS = CAPACITY // 128
FIELDS = 8
OWN_AT = 8
WINDOW = 96
PACKET = 24 + FIELDS * MARGIN_ROWS
FLOAT = jnp.float32


def lookup(row, lanes):
    wide = jnp.broadcast_to(row, (8, 128))
    return jnp.take_along_axis(wide, lanes, axis=1, mode="promise_in_bounds")


def kernel(
    members,
    density,
    gradient,
    elem_size,
    history,
    flags,
    neighbors,
    weights,
    ghost_send,
    counts,
    indicator,
    children,
    density_v,
    gradient_v,
    size_v,
    history_v,
    flags_v,
    neighbors_v,
    weights_v,
    ghost_v,
    counts_v,
    gradient_t,
    history_t,
    neighbors_t,
    weights_t,
    ghost_t,
    found,
    window,
    shifted,
    outgoing,
    incoming,
    local_sems,
    send_sems,
    recv_sems,
):
    me = lax.axis_index("dom")
    far = members // 8
    targets = [lax.rem(me + o + members, members) for o in (1, -1, far, -far)]

    pairs = (
        (gradient, gradient_v),
        (ghost_send, ghost_v),
        (density, density_v),
        (elem_size, size_v),
        (history, history_v),
        (flags, flags_v),
        (neighbors, neighbors_v),
        (counts, counts_v),
        (weights, weights_v),
    )
    copies = [
        pltpu.make_async_copy(source, target, local_sems.at[i])
        for i, (source, target) in enumerate(pairs)
    ]
    for copy in copies:
        copy.start()

    barrier = pltpu.get_barrier_semaphore()
    for target in targets:
        pl.semaphore_signal(
            barrier, inc=1, device_id=(target,), device_id_type=pl.DeviceIdType.MESH
        )

    copies[0].wait()
    copies[1].wait()
    for t in range(8):
        ghost_t[4 * t : 4 * t + 4, :] = ghost_v[:, 128 * t : 128 * t + 128]
    for k in range(4):
        index = ghost_t[pl.ds(k, 8, stride=4), :]
        lanes, rows = index & 127, index >> 7
        totals = [jnp.zeros((8, 128), FLOAT) for _ in range(3)]
        for r in range(ROWS):
            hit = rows == r
            for c in range(3):
                got = lookup(gradient_v[c : c + 1, 128 * r : 128 * r + 128], lanes)
                totals[c] = jnp.where(hit, got, totals[c])
        for c in range(3):
            outgoing[k, 8 * c : 8 * c + 8, :] = totals[c]

    for t in range(ROWS):
        gradient_t[4 * t : 4 * t + 3, :] = gradient_v[:, 128 * t : 128 * t + 128]
    for i in (2, 3, 4, 5):
        copies[i].wait()
    for t in range(ROWS):
        history_t[2 * t : 2 * t + 2, :] = history_v[:, 128 * t : 128 * t + 128]
    for b in range(BLOCKS):
        own = slice(8 * b, 8 * b + 8)
        at = slice(OWN_AT + 8 * b, OWN_AT + 8 * b + 8)
        window[0, at, :] = density_v[own, :]
        for c in range(3):
            window[1 + c, at, :] = gradient_t[pl.ds(32 * b + c, 8, stride=4), :]
        window[4, at, :] = 0.25 * size_v[own, :]
        for c in range(2):
            window[5 + c, at, :] = history_t[pl.ds(16 * b + c, 8, stride=2), :]
        window[7, at, :] = flags_v[own, :].astype(FLOAT)
    for f in range(FIELDS):
        at = 24 + MARGIN_ROWS * f
        last = OWN_AT + ROWS - MARGIN_ROWS
        outgoing[0, at : at + MARGIN_ROWS, :] = window[f, last : last + MARGIN_ROWS, :]
        outgoing[1, at : at + MARGIN_ROWS, :] = window[f, OWN_AT : OWN_AT + MARGIN_ROWS, :]

    pl.semaphore_wait(barrier, 4)
    sends = []
    for k in range(4):
        size = PACKET if k < 2 else 24
        sends.append(
            pltpu.make_async_remote_copy(
                src_ref=outgoing.at[k, pl.ds(0, size)],
                dst_ref=incoming.at[k, pl.ds(0, size)],
                send_sem=send_sems.at[k],
                recv_sem=recv_sems.at[k],
                device_id=(targets[k],),
                device_id_type=pl.DeviceIdType.MESH,
            )
        )
        sends[k].start()

    copies[6].wait()
    for t in range(ROWS):
        neighbors_t[8 * t : 8 * t + 6, :] = neighbors_v[:, 128 * t : 128 * t + 128]

    def own_rows(block, carry):
        base = pl.multiple_of(block * 64, 64)
        for m in range(6):
            index = neighbors_t[pl.ds(base + m, 8, stride=8), :]
            lanes, rows = index & 127, index >> 7
            totals = [jnp.zeros((8, 128), FLOAT) for _ in range(3)]
            for r in range(ROWS):
                hit = rows == r
                for c in range(3):
                    got = lookup(gradient_v[c : c + 1, 128 * r : 128 * r + 128], lanes)
                    totals[c] = jnp.where(hit, got, totals[c])
            for c in range(3):
                found[block, 8 * (3 * m + c) : 8 * (3 * m + c) + 8, :] = totals[c]
        return carry

    lax.fori_loop(0, BLOCKS, own_rows, 0)

    for send in sends:
        send.wait()
    copies[8].wait()
    for t in range(ROWS):
        weights_t[8 * t : 8 * t + 6, :] = weights_v[:, 128 * t : 128 * t + 128]

    def ghost_rows(block, carry):
        base = pl.multiple_of(block * 64, 64)
        own = [gradient_t[pl.ds(pl.multiple_of(block * 32, 32) + c, 8, stride=4), :] for c in range(3)]
        result = jnp.zeros((8, 128), FLOAT)
        for m in range(6):
            index = neighbors_t[pl.ds(base + m, 8, stride=8), :]
            lanes, rows = index & 127, index >> 7
            totals = [found[block, 8 * (3 * m + c) : 8 * (3 * m + c) + 8, :] for c in range(3)]
            for k in range(4):
                for s in range(8):
                    hit = rows == ROWS + 8 * k + s
                    for c in range(3):
                        got = lookup(incoming[k, 8 * c + s : 8 * c + s + 1, :], lanes)
                        totals[c] = jnp.where(hit, got, totals[c])
            square = None
            for c in range(3):
                jump = own[c] - totals[c]
                square = jump * jump if square is None else square + jump * jump
            result = result + weights_t[pl.ds(base + m, 8, stride=8), :] * square
        indicator[pl.ds(pl.multiple_of(block * 8, 8), 8), :] = result
        return carry

    lax.fori_loop(0, BLOCKS, ghost_rows, 0)

    for f in range(FIELDS):
        at = 24 + MARGIN_ROWS * f
        window[f, OWN_AT - MARGIN_ROWS : OWN_AT, :] = incoming[0, at : at + MARGIN_ROWS, :]
        right = OWN_AT + ROWS
        window[f, right : right + 8, :] = jnp.zeros((8, 128), FLOAT)
        window[f, right + 8 : right + 16, :] = jnp.zeros((8, 128), FLOAT)
        window[f, right : right + MARGIN_ROWS, :] = incoming[1, at : at + MARGIN_ROWS, :]
    copies[7].wait()
    owners = lax.broadcasted_iota(jnp.int32, (1, 128), 1)
    held = counts_v[...]
    begin = jnp.sum(jnp.where(owners < me, held, 0))
    count = jnp.sum(jnp.where(owners == me, held, 0))
    count = jnp.minimum(count, members * ELEMENTS - begin)
    start = jnp.clip(begin - me * ELEMENTS + MARGIN, 0, 2 * MARGIN)
    first, turn = start // 128, start % 128
    first = first + OWN_AT - MARGIN_ROWS
    lane = lax.broadcasted_iota(jnp.int32, (8, 128), 1)
    slot = lax.broadcasted_iota(jnp.int32, (8, 128), 0) * 128 + lane
    turned = (lane + turn) & 127
    low = lane < 128 - turn
    for f in range(FIELDS):
        for b in range(OUT_ROWS // 8):
            here = window[f, pl.ds(first + 8 * b, 8), :]
            there = window[f, pl.ds(first + 8 * b + 1, 8), :]
            both = [jnp.take_along_axis(v, turned, axis=1, mode="promise_in_bounds") for v in (here, there)]
            value = jnp.where(low, both[0], both[1])
            if f in (0, 5, 6, 7):
                value = jnp.where(slot + 1024 * b < count, value, 0.0)
            shifted[f, 8 * b : 8 * b + 8, :] = value

    child = lax.broadcasted_iota(jnp.int32, (8, 128), 0)
    signs = [(2 * ((child >> c) & 1) - 1).astype(FLOAT) for c in range(3)]
    eldest = child == 0
    for t in range(OUT_ROWS):
        row = [jnp.broadcast_to(shifted[f, t : t + 1, :], (8, 128)) for f in range(FIELDS)]
        slope = signs[0] * row[1] + signs[1] * row[2] + signs[2] * row[3]
        refined = row[7] > 0.0
        kept = jnp.logical_or(refined, eldest)
        at = slice(128 * t, 128 * t + 128)
        moved = jnp.where(refined, row[0] + row[4] * slope, row[0])
        children[0, :, at] = jnp.where(kept, moved, 0.0)
        children[1, :, at] = jnp.where(kept, row[5], 0.0)
        children[2, :, at] = jnp.where(kept, row[6], 0.0)


def local(
    members,
    density,
    gradient,
    elem_size,
    history,
    refine_flags,
    face_neighbor,
    face_weight,
    ghost_send,
    new_counts,
):
    vmem = pltpu.VMEM
    flat = (ROWS, 128)
    indicator, children = pl.pallas_call(
        functools.partial(kernel, members),
        out_shape=(
            jax.ShapeDtypeStruct(flat, FLOAT),
            jax.ShapeDtypeStruct((3, 8, CAPACITY), FLOAT),
        ),
        in_specs=[pl.BlockSpec(memory_space=pl.ANY)] * 9,
        out_specs=(pl.BlockSpec(memory_space=vmem),) * 2,
        scratch_shapes=[
            vmem(flat, FLOAT),
            vmem((3, ELEMENTS), FLOAT),
            vmem(flat, FLOAT),
            vmem((2, ELEMENTS), FLOAT),
            vmem(flat, jnp.int32),
            vmem((6, ELEMENTS), jnp.int32),
            vmem((6, ELEMENTS), FLOAT),
            vmem((4, GHOST), jnp.int32),
            vmem((1, 128), jnp.int32),
            vmem((4 * ROWS, 128), FLOAT),
            vmem((2 * ROWS, 128), FLOAT),
            vmem((8 * ROWS, 128), jnp.int32),
            vmem((8 * ROWS, 128), FLOAT),
            vmem((32, 128), jnp.int32),
            vmem((BLOCKS, 144, 128), FLOAT),
            vmem((FIELDS, WINDOW, 128), FLOAT),
            vmem((FIELDS, OUT_ROWS, 128), FLOAT),
            vmem((4, PACKET, 128), FLOAT),
            vmem((4, PACKET, 128), FLOAT),
            pltpu.SemaphoreType.DMA((9,)),
            pltpu.SemaphoreType.DMA((4,)),
            pltpu.SemaphoreType.DMA((4,)),
        ],
        compiler_params=pltpu.CompilerParams(
            collective_id=0, has_side_effects=True, vmem_limit_bytes=32 * 1024 * 1024
        ),
    )(
        density.reshape(flat),
        gradient,
        elem_size.reshape(flat),
        history,
        refine_flags.reshape(flat),
        face_neighbor,
        face_weight,
        ghost_send,
        new_counts.reshape(1, 128),
    )
    return indicator.reshape(ELEMENTS), children


def solution(mesh):
    placed = (
        P("dom"),
        P(None, "dom"),
        P("dom"),
        P(None, "dom"),
        P("dom"),
        P(None, "dom"),
        P(None, "dom"),
        P("dom", None),
        P(),
    )
    return jax.shard_map(
        functools.partial(local, mesh.shape["dom"]),
        mesh=mesh,
        in_specs=placed,
        out_specs=(P("dom"), P(None, None, "dom")),
        check_vma=False,
    )
```

```python
import functools

import jax
import jax.numpy as jnp
from jax import lax
from jax.experimental import pallas as pl
from jax.experimental.pallas import tpu as pltpu
from jax.sharding import PartitionSpec as P

ELEMENTS = 8192
ROWS = ELEMENTS // 128
BLOCKS = ROWS // 8
GHOST = 1024
MARGIN = 512
MARGIN_ROWS = MARGIN // 128
CAPACITY = ELEMENTS + 2 * MARGIN
OUT_ROWS = CAPACITY // 128
FIELDS = 8
OWN_AT = 8
WINDOW = 96
PACKET = 24 + FIELDS * MARGIN_ROWS
FLOAT = jnp.float32


def lookup(row, lanes):
    wide = jnp.broadcast_to(row, (8, 128))
    return jnp.take_along_axis(wide, lanes, axis=1, mode="promise_in_bounds")


def kernel(
    members,
    density,
    gradient,
    elem_size,
    history,
    flags,
    neighbors,
    weights,
    ghost_send,
    counts,
    indicator,
    children,
    density_v,
    gradient_v,
    size_v,
    history_v,
    flags_v,
    neighbors_v,
    weights_v,
    ghost_v,
    counts_v,
    gradient_t,
    history_t,
    neighbors_t,
    weights_t,
    ghost_t,
    found,
    window,
    shifted,
    outgoing,
    incoming,
    local_sems,
    send_sems,
    recv_sems,
):
    me = lax.axis_index("dom")
    far = members // 8
    targets = [lax.rem(me + o + members, members) for o in (1, -1, far, -far)]

    pairs = (
        (gradient, gradient_v),
        (ghost_send, ghost_v),
        (density, density_v),
        (elem_size, size_v),
        (history, history_v),
        (flags, flags_v),
        (neighbors, neighbors_v),
        (counts, counts_v),
        (weights, weights_v),
    )
    copies = [
        pltpu.make_async_copy(source, target, local_sems.at[i])
        for i, (source, target) in enumerate(pairs)
    ]
    for copy in copies:
        copy.start()

    barrier = pltpu.get_barrier_semaphore()
    for target in targets:
        pl.semaphore_signal(
            barrier, inc=1, device_id=(target,), device_id_type=pl.DeviceIdType.MESH
        )

    copies[0].wait()
    copies[1].wait()
    for t in range(8):
        ghost_t[4 * t : 4 * t + 4, :] = ghost_v[:, 128 * t : 128 * t + 128]
    for k in range(4):
        index = ghost_t[pl.ds(k, 8, stride=4), :]
        lanes, rows = index & 127, index >> 7
        totals = [jnp.zeros((8, 128), FLOAT) for _ in range(3)]
        for r in range(ROWS):
            hit = rows == r
            for c in range(3):
                got = lookup(gradient_v[c : c + 1, 128 * r : 128 * r + 128], lanes)
                totals[c] = jnp.where(hit, got, totals[c])
        for c in range(3):
            outgoing[k, 8 * c : 8 * c + 8, :] = totals[c]

    for t in range(ROWS):
        gradient_t[4 * t : 4 * t + 3, :] = gradient_v[:, 128 * t : 128 * t + 128]
    for i in (2, 3, 4, 5):
        copies[i].wait()
    for t in range(ROWS):
        history_t[2 * t : 2 * t + 2, :] = history_v[:, 128 * t : 128 * t + 128]
    for b in range(BLOCKS):
        own = slice(8 * b, 8 * b + 8)
        at = slice(OWN_AT + 8 * b, OWN_AT + 8 * b + 8)
        window[0, at, :] = density_v[own, :]
        for c in range(3):
            window[1 + c, at, :] = gradient_t[pl.ds(32 * b + c, 8, stride=4), :]
        window[4, at, :] = 0.25 * size_v[own, :]
        for c in range(2):
            window[5 + c, at, :] = history_t[pl.ds(16 * b + c, 8, stride=2), :]
        window[7, at, :] = flags_v[own, :].astype(FLOAT)
    for f in range(FIELDS):
        at = 24 + MARGIN_ROWS * f
        last = OWN_AT + ROWS - MARGIN_ROWS
        outgoing[0, at : at + MARGIN_ROWS, :] = window[f, last : last + MARGIN_ROWS, :]
        outgoing[1, at : at + MARGIN_ROWS, :] = window[f, OWN_AT : OWN_AT + MARGIN_ROWS, :]

    pl.semaphore_wait(barrier, 4)
    sends = []
    for k in range(4):
        size = PACKET if k < 2 else 24
        sends.append(
            pltpu.make_async_remote_copy(
                src_ref=outgoing.at[k, pl.ds(0, size)],
                dst_ref=incoming.at[k, pl.ds(0, size)],
                send_sem=send_sems.at[k],
                recv_sem=recv_sems.at[k],
                device_id=(targets[k],),
                device_id_type=pl.DeviceIdType.MESH,
            )
        )
        sends[k].start()

    copies[6].wait()
    for t in range(ROWS):
        neighbors_t[8 * t : 8 * t + 6, :] = neighbors_v[:, 128 * t : 128 * t + 128]

    def own_rows(block, carry):
        base = pl.multiple_of(block * 64, 64)
        for m in range(6):
            index = neighbors_t[pl.ds(base + m, 8, stride=8), :]
            lanes, rows = index & 127, index >> 7
            totals = [jnp.zeros((8, 128), FLOAT) for _ in range(3)]
            for r in range(ROWS):
                hit = rows == r
                for c in range(3):
                    got = lookup(gradient_v[c : c + 1, 128 * r : 128 * r + 128], lanes)
                    totals[c] = jnp.where(hit, got, totals[c])
            for c in range(3):
                found[block, 8 * (3 * m + c) : 8 * (3 * m + c) + 8, :] = totals[c]
        return carry

    lax.fori_loop(0, BLOCKS, own_rows, 0)

    for send in sends:
        send.wait()
    copies[8].wait()
    for t in range(ROWS):
        weights_t[8 * t : 8 * t + 6, :] = weights_v[:, 128 * t : 128 * t + 128]

    def ghost_rows(block, carry):
        base = pl.multiple_of(block * 64, 64)
        own = [gradient_t[pl.ds(pl.multiple_of(block * 32, 32) + c, 8, stride=4), :] for c in range(3)]
        result = jnp.zeros((8, 128), FLOAT)
        for m in range(6):
            index = neighbors_t[pl.ds(base + m, 8, stride=8), :]
            lanes, rows = index & 127, index >> 7
            totals = [found[block, 8 * (3 * m + c) : 8 * (3 * m + c) + 8, :] for c in range(3)]
            for k in range(4):
                for s in range(8):
                    hit = rows == ROWS + 8 * k + s
                    for c in range(3):
                        got = lookup(incoming[k, 8 * c + s : 8 * c + s + 1, :], lanes)
                        totals[c] = jnp.where(hit, got, totals[c])
            square = None
            for c in range(3):
                jump = own[c] - totals[c]
                square = jump * jump if square is None else square + jump * jump
            result = result + weights_t[pl.ds(base + m, 8, stride=8), :] * square
        indicator[pl.ds(pl.multiple_of(block * 8, 8), 8), :] = result
        return carry

    lax.fori_loop(0, BLOCKS, ghost_rows, 0)

    for f in range(FIELDS):
        at = 24 + MARGIN_ROWS * f
        window[f, OWN_AT - MARGIN_ROWS : OWN_AT, :] = incoming[0, at : at + MARGIN_ROWS, :]
        right = OWN_AT + ROWS
        window[f, right : right + 8, :] = jnp.zeros((8, 128), FLOAT)
        window[f, right + 8 : right + 16, :] = jnp.zeros((8, 128), FLOAT)
        window[f, right : right + MARGIN_ROWS, :] = incoming[1, at : at + MARGIN_ROWS, :]
    copies[7].wait()
    owners = lax.broadcasted_iota(jnp.int32, (1, 128), 1)
    held = counts_v[...]
    begin = jnp.sum(jnp.where(owners < me, held, 0))
    count = jnp.sum(jnp.where(owners == me, held, 0))
    count = jnp.minimum(count, members * ELEMENTS - begin)
    start = jnp.clip(begin - me * ELEMENTS + MARGIN, 0, 2 * MARGIN)
    first, turn = start // 128, start % 128
    first = first + OWN_AT - MARGIN_ROWS
    lane = lax.broadcasted_iota(jnp.int32, (8, 128), 1)
    slot = lax.broadcasted_iota(jnp.int32, (8, 128), 0) * 128 + lane
    turned = (lane + turn) & 127
    low = lane < 128 - turn
    for f in range(FIELDS):
        for b in range(OUT_ROWS // 8):
            here = window[f, pl.ds(first + 8 * b, 8), :]
            there = window[f, pl.ds(first + 8 * b + 1, 8), :]
            both = [jnp.take_along_axis(v, turned, axis=1, mode="promise_in_bounds") for v in (here, there)]
            value = jnp.where(low, both[0], both[1])
            if f in (0, 5, 6, 7):
                value = jnp.where(slot + 1024 * b < count, value, 0.0)
            shifted[f, 8 * b : 8 * b + 8, :] = value

    child = lax.broadcasted_iota(jnp.int32, (8, 128), 0)
    signs = [(2 * ((child >> c) & 1) - 1).astype(FLOAT) for c in range(3)]
    eldest = child == 0
    for t in range(OUT_ROWS):
        row = [jnp.broadcast_to(shifted[f, t : t + 1, :], (8, 128)) for f in range(FIELDS)]
        slope = signs[0] * row[1] + signs[1] * row[2] + signs[2] * row[3]
        refined = row[7] > 0.0
        kept = jnp.logical_or(refined, eldest)
        at = slice(128 * t, 128 * t + 128)
        moved = jnp.where(refined, row[0] + row[4] * slope, row[0])
        children[0, :, at] = jnp.where(kept, moved, 0.0)
        children[1, :, at] = jnp.where(kept, row[5], 0.0)
        children[2, :, at] = jnp.where(kept, row[6], 0.0)


def local(
    members,
    density,
    gradient,
    elem_size,
    history,
    refine_flags,
    face_neighbor,
    face_weight,
    ghost_send,
    new_counts,
):
    vmem = pltpu.VMEM
    flat = (ROWS, 128)
    operands = (
        density.reshape(flat),
        gradient,
        elem_size.reshape(flat),
        history,
        refine_flags.reshape(flat),
        face_neighbor,
        face_weight,
        ghost_send,
        new_counts.reshape(1, 128),
    )
    operands = [pltpu.with_memory_space_constraint(x, pltpu.HBM) for x in operands]
    indicator, children = pl.pallas_call(
        functools.partial(kernel, members),
        out_shape=(
            jax.ShapeDtypeStruct(flat, FLOAT),
            jax.ShapeDtypeStruct((3, 8, CAPACITY), FLOAT),
        ),
        in_specs=[pl.BlockSpec(memory_space=pltpu.HBM)] * 9,
        out_specs=(pl.BlockSpec(memory_space=vmem),) * 2,
        scratch_shapes=[
            vmem(flat, FLOAT),
            vmem((3, ELEMENTS), FLOAT),
            vmem(flat, FLOAT),
            vmem((2, ELEMENTS), FLOAT),
            vmem(flat, jnp.int32),
            vmem((6, ELEMENTS), jnp.int32),
            vmem((6, ELEMENTS), FLOAT),
            vmem((4, GHOST), jnp.int32),
            vmem((1, 128), jnp.int32),
            vmem((4 * ROWS, 128), FLOAT),
            vmem((2 * ROWS, 128), FLOAT),
            vmem((8 * ROWS, 128), jnp.int32),
            vmem((8 * ROWS, 128), FLOAT),
            vmem((32, 128), jnp.int32),
            vmem((BLOCKS, 144, 128), FLOAT),
            vmem((FIELDS, WINDOW, 128), FLOAT),
            vmem((FIELDS, OUT_ROWS, 128), FLOAT),
            vmem((4, PACKET, 128), FLOAT),
            vmem((4, PACKET, 128), FLOAT),
            pltpu.SemaphoreType.DMA((9,)),
            pltpu.SemaphoreType.DMA((4,)),
            pltpu.SemaphoreType.DMA((4,)),
        ],
        compiler_params=pltpu.CompilerParams(
            collective_id=0, has_side_effects=True, vmem_limit_bytes=32 * 1024 * 1024
        ),
    )(*operands)
    return indicator.reshape(ELEMENTS), children


def solution(mesh):
    placed = (
        P("dom"),
        P(None, "dom"),
        P("dom"),
        P(None, "dom"),
        P("dom"),
        P(None, "dom"),
        P(None, "dom"),
        P("dom", None),
        P(),
    )
    return jax.shard_map(
        functools.partial(local, mesh.shape["dom"]),
        mesh=mesh,
        in_specs=placed,
        out_specs=(P("dom"), P(None, None, "dom")),
        check_vma=False,
    )
```

```python
import functools

import jax
import jax.numpy as jnp
from jax import lax
from jax.experimental import pallas as pl
from jax.experimental.pallas import tpu as pltpu
from jax.sharding import PartitionSpec as P

ELEMENTS = 8192
ROWS = ELEMENTS // 128
BLOCKS = ROWS // 8
GHOST = 1024
MARGIN = 512
MARGIN_ROWS = MARGIN // 128
CAPACITY = ELEMENTS + 2 * MARGIN
OUT_ROWS = CAPACITY // 128
FIELDS = 8
OWN_AT = 8
WINDOW = 96
PACKET = 24 + FIELDS * MARGIN_ROWS
FLOAT = jnp.float32


def lookup(row, lanes):
    wide = jnp.broadcast_to(row, (8, 128))
    return jnp.take_along_axis(wide, lanes, axis=1, mode="promise_in_bounds")


def kernel(
    members,
    density,
    gradient,
    elem_size,
    history,
    flags,
    neighbors,
    weights,
    ghost_send,
    counts,
    indicator,
    children,
    density_v,
    gradient_v,
    size_v,
    history_v,
    flags_v,
    neighbors_v,
    weights_v,
    ghost_v,
    counts_v,
    gradient_t,
    history_t,
    neighbors_t,
    weights_t,
    ghost_t,
    column_t,
    row_t,
    table,
    steps,
    own_sum,
    terms,
    window,
    shifted,
    outgoing,
    incoming,
    local_sems,
    send_sems,
    recv_sems,
):
    me = lax.axis_index("dom")
    far = members // 8
    targets = [lax.rem(me + o + members, members) for o in (1, -1, far, -far)]

    pairs = (
        (gradient, gradient_v),
        (ghost_send, ghost_v),
        (density, density_v),
        (elem_size, size_v),
        (history, history_v),
        (flags, flags_v),
        (neighbors, neighbors_v),
        (counts, counts_v),
        (weights, weights_v),
    )
    copies = [
        pltpu.make_async_copy(source, target, local_sems.at[i])
        for i, (source, target) in enumerate(pairs)
    ]
    for copy in copies:
        copy.start()

    barrier = pltpu.get_barrier_semaphore()
    for target in targets:
        pl.semaphore_signal(
            barrier, inc=1, device_id=(target,), device_id_type=pl.DeviceIdType.MESH
        )

    copies[0].wait()
    copies[1].wait()
    for t in range(8):
        ghost_t[4 * t : 4 * t + 4, :] = ghost_v[:, 128 * t : 128 * t + 128]
    for k in range(4):
        index = ghost_t[pl.ds(k, 8, stride=4), :]
        lanes, rows = index & 127, index >> 7
        totals = [jnp.zeros((8, 128), FLOAT) for _ in range(3)]
        for r in range(ROWS):
            hit = rows == r
            for c in range(3):
                got = lookup(gradient_v[c : c + 1, 128 * r : 128 * r + 128], lanes)
                totals[c] = jnp.where(hit, got, totals[c])
        for c in range(3):
            outgoing[k, 8 * c : 8 * c + 8, :] = totals[c]

    for t in range(ROWS):
        gradient_t[4 * t : 4 * t + 3, :] = gradient_v[:, 128 * t : 128 * t + 128]
    for i in (2, 3, 4, 5):
        copies[i].wait()
    for t in range(ROWS):
        history_t[2 * t : 2 * t + 2, :] = history_v[:, 128 * t : 128 * t + 128]
    for b in range(BLOCKS):
        own = slice(8 * b, 8 * b + 8)
        at = slice(OWN_AT + 8 * b, OWN_AT + 8 * b + 8)
        window[0, at, :] = density_v[own, :]
        for c in range(3):
            window[1 + c, at, :] = gradient_t[pl.ds(32 * b + c, 8, stride=4), :]
        window[4, at, :] = 0.25 * size_v[own, :]
        for c in range(2):
            window[5 + c, at, :] = history_t[pl.ds(16 * b + c, 8, stride=2), :]
        window[7, at, :] = flags_v[own, :].astype(FLOAT)
    for f in range(FIELDS):
        at = 24 + MARGIN_ROWS * f
        last = OWN_AT + ROWS - MARGIN_ROWS
        outgoing[0, at : at + MARGIN_ROWS, :] = window[f, last : last + MARGIN_ROWS, :]
        outgoing[1, at : at + MARGIN_ROWS, :] = window[f, OWN_AT : OWN_AT + MARGIN_ROWS, :]

    pl.semaphore_wait(barrier, 4)
    sends = []
    for k in range(4):
        size = PACKET if k < 2 else 24
        sends.append(
            pltpu.make_async_remote_copy(
                src_ref=outgoing.at[k, pl.ds(0, size)],
                dst_ref=incoming.at[k, pl.ds(0, size)],
                send_sem=send_sems.at[k],
                recv_sem=recv_sems.at[k],
                device_id=(targets[k],),
                device_id_type=pl.DeviceIdType.MESH,
            )
        )
        sends[k].start()

    copies[6].wait()
    copies[8].wait()
    for t in range(ROWS):
        index = neighbors_v[:, 128 * t : 128 * t + 128]
        neighbors_t[8 * t : 8 * t + 6, :] = index
        half = (index >> 12) & 1
        column_t[8 * t : 8 * t + 6, :] = ((index & 127) + 128 * half + 256 * (index >> 13)).astype(FLOAT)
        row_t[8 * t : 8 * t + 6, :] = (index >> 7) & 31
        weights_t[8 * t : 8 * t + 6, :] = weights_v[:, 128 * t : 128 * t + 128]
    for c in range(3):
        for half in range(2):
            for q in range(2):
                part = jnp.concatenate(
                    [gradient_t[pl.ds(4 * (32 * half + 16 * q + 8 * u) + c, 8, stride=4), :] for u in range(2)], axis=0
                )
                for s in range(3):
                    piece = part.astype(jnp.bfloat16)
                    at = 96 * s + 32 * c + 16 * q
                    table[at : at + 16, 128 * half : 128 * half + 128] = piece
                    part = part - piece.astype(FLOAT)
    steps[...] = lax.broadcasted_iota(jnp.int32, (256, 128), 0).astype(FLOAT).astype(jnp.bfloat16)
    sublane = lax.broadcasted_iota(jnp.int32, (8, 128), 0)
    one, zero = jnp.ones((), jnp.bfloat16), jnp.zeros((), jnp.bfloat16)

    def wide(ref, at):
        return jnp.broadcast_to(ref[pl.ds(at, 1), :], (8, 128))

    def own_block(block):
        for p in range(4):
            sums = [jnp.zeros((8, 128), FLOAT) for _ in range(2)]
            rows = [8 * block + 2 * p + e for e in range(2)]
            for m in range(6):
                hot = []
                for e in range(2):
                    column = jnp.broadcast_to(column_t[pl.ds(8 * rows[e] + m, 1), :], (16, 128))
                    column = jnp.concatenate([column.astype(jnp.bfloat16)] * 16, axis=0)
                    hot.append(jnp.where(column == steps[...], one, zero))
                hot = jnp.concatenate(hot, axis=1)
                got = jnp.dot(table[...], hot, preferred_element_type=FLOAT)
                got = got[0:96] + got[96:192] + got[192:288]
                for e in range(2):
                    row = wide(row_t, 8 * rows[e] + m)
                    hits = [row == sublane + 8 * g for g in range(4)]
                    square = None
                    for c in range(3):
                        value = jnp.zeros((8, 128), FLOAT)
                        for g in range(4):
                            at = 32 * c + 8 * g
                            value = jnp.where(hits[g], got[at : at + 8, 128 * e : 128 * e + 128], value)
                        jump = wide(gradient_t, 4 * rows[e] + c) - value
                        square = jump * jump if square is None else square + jump * jump
                    here = jnp.logical_and((row & 7) == sublane, wide(column_t, 8 * rows[e] + m) < 256.0)
                    sums[e] = sums[e] + jnp.where(here, wide(weights_t, 8 * rows[e] + m) * square, 0.0)
            for e in range(2):
                own_sum[pl.ds(rows[e], 1), :] = jnp.sum(sums[e], axis=0, keepdims=True)

    def ghost_unit(unit, odd):
        block = unit // 6
        m = unit - 6 * block
        base = pl.multiple_of(block * 64, 64)
        index = neighbors_t[pl.ds(base + m, 8, stride=8), :]
        lanes, rows = index & 127, index >> 7
        totals = [jnp.zeros((8, 128), FLOAT) for _ in range(3)]
        for k in (odd, 2 + odd):
            for s in range(8):
                hit = rows == ROWS + 8 * k + s
                for c in range(3):
                    got = lookup(incoming[k, 8 * c + s : 8 * c + s + 1, :], lanes)
                    totals[c] = jnp.where(hit, got, totals[c])
        square = None
        for c in range(3):
            jump = gradient_t[pl.ds(pl.multiple_of(block * 32, 32) + c, 8, stride=4), :] - totals[c]
            square = jump * jump if square is None else square + jump * jump
        here = jnp.logical_and(rows >= ROWS, ((rows >> 3) & 1) == odd)
        terms[odd, unit] = jnp.where(here, weights_t[pl.ds(base + m, 8, stride=8), :] * square, 0.0)

    def alone(block, carry):
        own_block(block)
        return carry

    def beside(odd, first_block, step, carry):
        for v in range(16):
            ghost_unit(16 * step + v, odd)
        own_block(first_block + step)
        return carry

    lax.fori_loop(0, 2, alone, 0)
    sends[1].wait_recv()
    sends[3].wait_recv()
    lax.fori_loop(0, 3, functools.partial(beside, 1, 2), 0)
    sends[0].wait_recv()
    sends[2].wait_recv()
    lax.fori_loop(0, 3, functools.partial(beside, 0, 5), 0)
    for block in range(BLOCKS):
        total = own_sum[8 * block : 8 * block + 8, :]
        for m in range(6):
            total = total + (terms[0, 6 * block + m] + terms[1, 6 * block + m])
        indicator[8 * block : 8 * block + 8, :] = total

    for f in range(FIELDS):
        at = 24 + MARGIN_ROWS * f
        window[f, OWN_AT - MARGIN_ROWS : OWN_AT, :] = incoming[0, at : at + MARGIN_ROWS, :]
        right = OWN_AT + ROWS
        window[f, right : right + 8, :] = jnp.zeros((8, 128), FLOAT)
        window[f, right + 8 : right + 16, :] = jnp.zeros((8, 128), FLOAT)
        window[f, right : right + MARGIN_ROWS, :] = incoming[1, at : at + MARGIN_ROWS, :]
    copies[7].wait()
    owners = lax.broadcasted_iota(jnp.int32, (1, 128), 1)
    held = counts_v[...]
    begin = jnp.sum(jnp.where(owners < me, held, 0))
    count = jnp.sum(jnp.where(owners == me, held, 0))
    count = jnp.minimum(count, members * ELEMENTS - begin)
    start = jnp.clip(begin - me * ELEMENTS + MARGIN, 0, 2 * MARGIN)
    first, turn = start // 128, start % 128
    first = first + OWN_AT - MARGIN_ROWS
    lane = lax.broadcasted_iota(jnp.int32, (8, 128), 1)
    slot = lax.broadcasted_iota(jnp.int32, (8, 128), 0) * 128 + lane
    turned = (lane + turn) & 127
    low = lane < 128 - turn
    for f in range(FIELDS):
        for b in range(OUT_ROWS // 8):
            here = window[f, pl.ds(first + 8 * b, 8), :]
            there = window[f, pl.ds(first + 8 * b + 1, 8), :]
            both = [jnp.take_along_axis(v, turned, axis=1, mode="promise_in_bounds") for v in (here, there)]
            value = jnp.where(low, both[0], both[1])
            if f in (0, 5, 6, 7):
                value = jnp.where(slot + 1024 * b < count, value, 0.0)
            shifted[f, 8 * b : 8 * b + 8, :] = value

    child = lax.broadcasted_iota(jnp.int32, (8, 128), 0)
    signs = [(2 * ((child >> c) & 1) - 1).astype(FLOAT) for c in range(3)]
    eldest = child == 0
    for t in range(OUT_ROWS):
        row = [jnp.broadcast_to(shifted[f, t : t + 1, :], (8, 128)) for f in range(FIELDS)]
        slope = signs[0] * row[1] + signs[1] * row[2] + signs[2] * row[3]
        refined = row[7] > 0.0
        kept = jnp.logical_or(refined, eldest)
        at = slice(128 * t, 128 * t + 128)
        moved = jnp.where(refined, row[0] + row[4] * slope, row[0])
        children[0, :, at] = jnp.where(kept, moved, 0.0)
        children[1, :, at] = jnp.where(kept, row[5], 0.0)
        children[2, :, at] = jnp.where(kept, row[6], 0.0)
    for send in sends:
        send.wait_send()


def local(
    members,
    density,
    gradient,
    elem_size,
    history,
    refine_flags,
    face_neighbor,
    face_weight,
    ghost_send,
    new_counts,
):
    vmem = pltpu.VMEM
    flat = (ROWS, 128)
    operands = (
        density.reshape(flat),
        gradient,
        elem_size.reshape(flat),
        history,
        refine_flags.reshape(flat),
        face_neighbor,
        face_weight,
        ghost_send,
        new_counts.reshape(1, 128),
    )
    operands = [pltpu.with_memory_space_constraint(x, pltpu.HBM) for x in operands]
    indicator, children = pl.pallas_call(
        functools.partial(kernel, members),
        out_shape=(
            jax.ShapeDtypeStruct(flat, FLOAT),
            jax.ShapeDtypeStruct((3, 8, CAPACITY), FLOAT),
        ),
        in_specs=[pl.BlockSpec(memory_space=pltpu.HBM)] * 9,
        out_specs=(pl.BlockSpec(memory_space=vmem),) * 2,
        scratch_shapes=[
            vmem(flat, FLOAT),
            vmem((3, ELEMENTS), FLOAT),
            vmem(flat, FLOAT),
            vmem((2, ELEMENTS), FLOAT),
            vmem(flat, jnp.int32),
            vmem((6, ELEMENTS), jnp.int32),
            vmem((6, ELEMENTS), FLOAT),
            vmem((4, GHOST), jnp.int32),
            vmem((1, 128), jnp.int32),
            vmem((4 * ROWS, 128), FLOAT),
            vmem((2 * ROWS, 128), FLOAT),
            vmem((8 * ROWS, 128), jnp.int32),
            vmem((8 * ROWS, 128), FLOAT),
            vmem((32, 128), jnp.int32),
            vmem((8 * ROWS, 128), FLOAT),
            vmem((8 * ROWS, 128), jnp.int32),
            vmem((288, 256), jnp.bfloat16),
            vmem((256, 128), jnp.bfloat16),
            vmem(flat, FLOAT),
            vmem((2, 6 * BLOCKS, 8, 128), FLOAT),
            vmem((FIELDS, WINDOW, 128), FLOAT),
            vmem((FIELDS, OUT_ROWS, 128), FLOAT),
            vmem((4, PACKET, 128), FLOAT),
            vmem((4, PACKET, 128), FLOAT),
            pltpu.SemaphoreType.DMA((9,)),
            pltpu.SemaphoreType.DMA((4,)),
            pltpu.SemaphoreType.DMA((4,)),
        ],
        compiler_params=pltpu.CompilerParams(
            collective_id=0, has_side_effects=True, vmem_limit_bytes=32 * 1024 * 1024
        ),
    )(*operands)
    return indicator.reshape(ELEMENTS), children


def solution(mesh):
    placed = (
        P("dom"),
        P(None, "dom"),
        P("dom"),
        P(None, "dom"),
        P("dom"),
        P(None, "dom"),
        P(None, "dom"),
        P("dom", None),
        P(),
    )
    return jax.shard_map(
        functools.partial(local, mesh.shape["dom"]),
        mesh=mesh,
        in_specs=placed,
        out_specs=(P("dom"), P(None, None, "dom")),
        check_vma=False,
    )
```

```python
import functools

import jax
import jax.numpy as jnp
from jax import lax
from jax.experimental import pallas as pl
from jax.experimental.pallas import tpu as pltpu
from jax.sharding import PartitionSpec as P

ELEMENTS = 8192
ROWS = ELEMENTS // 128
BLOCKS = ROWS // 8
GHOST = 1024
MARGIN = 512
MARGIN_ROWS = MARGIN // 128
CAPACITY = ELEMENTS + 2 * MARGIN
OUT_ROWS = CAPACITY // 128
FIELDS = 8
OWN_AT = 8
WINDOW = 96
PACKET = 24 + FIELDS * MARGIN_ROWS
FLOAT = jnp.float32


def lookup(row, lanes):
    wide = jnp.broadcast_to(row, (8, 128))
    return jnp.take_along_axis(wide, lanes, axis=1, mode="promise_in_bounds")


def kernel(
    members,
    density,
    gradient,
    elem_size,
    history,
    flags,
    neighbors,
    weights,
    ghost_send,
    counts,
    indicator,
    children,
    density_v,
    gradient_v,
    size_v,
    history_v,
    flags_v,
    neighbors_v,
    weights_v,
    ghost_v,
    counts_v,
    gradient_t,
    history_t,
    neighbors_t,
    weights_t,
    ghost_t,
    column_t,
    row_t,
    table,
    steps,
    own_sum,
    terms,
    window,
    shifted,
    outgoing,
    incoming,
    local_sems,
    send_sems,
    recv_sems,
    ready_sems,
):
    me = lax.axis_index("dom")
    far = members // 8
    targets = [lax.rem(me + o + members, members) for o in (1, -1, far, -far)]

    pairs = (
        (gradient, gradient_v),
        (ghost_send, ghost_v),
        (density, density_v),
        (elem_size, size_v),
        (history, history_v),
        (flags, flags_v),
        (neighbors, neighbors_v),
        (counts, counts_v),
        (weights, weights_v),
    )
    copies = [
        pltpu.make_async_copy(source, target, local_sems.at[i])
        for i, (source, target) in enumerate(pairs)
    ]
    for copy in copies[:2]:
        copy.start()

    offsets = (1, -1, far, -far)
    mesh_id = pl.DeviceIdType.MESH
    barrier = pltpu.get_barrier_semaphore()
    for k in range(4):
        announce = functools.partial(
            pl.semaphore_signal, barrier, inc=1, device_id=(targets[k],), device_id_type=mesh_id
        )
        if offsets[k] > 0:
            pl.when(me + offsets[k] < members)(announce)
        else:
            announce()
    for copy in copies[2:]:
        copy.start()

    copies[0].wait()
    copies[1].wait()
    for t in range(8):
        ghost_t[4 * t : 4 * t + 4, :] = ghost_v[:, 128 * t : 128 * t + 128]
    for k in range(4):
        index = ghost_t[pl.ds(k, 8, stride=4), :]
        lanes, rows = index & 127, index >> 7
        totals = [jnp.zeros((8, 128), FLOAT) for _ in range(3)]
        for r in range(ROWS):
            hit = rows == r
            for c in range(3):
                got = lookup(gradient_v[c : c + 1, 128 * r : 128 * r + 128], lanes)
                totals[c] = jnp.where(hit, got, totals[c])
        for c in range(3):
            outgoing[k, 8 * c : 8 * c + 8, :] = totals[c]

    for t in range(ROWS):
        gradient_t[4 * t : 4 * t + 3, :] = gradient_v[:, 128 * t : 128 * t + 128]
    for i in (2, 3, 4, 5):
        copies[i].wait()
    for t in range(ROWS):
        history_t[2 * t : 2 * t + 2, :] = history_v[:, 128 * t : 128 * t + 128]
    for b in range(BLOCKS):
        own = slice(8 * b, 8 * b + 8)
        at = slice(OWN_AT + 8 * b, OWN_AT + 8 * b + 8)
        window[0, at, :] = density_v[own, :]
        for c in range(3):
            window[1 + c, at, :] = gradient_t[pl.ds(32 * b + c, 8, stride=4), :]
        window[4, at, :] = 0.25 * size_v[own, :]
        for c in range(2):
            window[5 + c, at, :] = history_t[pl.ds(16 * b + c, 8, stride=2), :]
        window[7, at, :] = flags_v[own, :].astype(FLOAT)
    for f in range(FIELDS):
        at = 24 + MARGIN_ROWS * f
        last = OWN_AT + ROWS - MARGIN_ROWS
        outgoing[0, at : at + MARGIN_ROWS, :] = window[f, last : last + MARGIN_ROWS, :]
        outgoing[1, at : at + MARGIN_ROWS, :] = window[f, OWN_AT : OWN_AT + MARGIN_ROWS, :]

    pl.semaphore_wait(barrier, 4 - (me < far).astype(jnp.int32) - (me < 1).astype(jnp.int32))
    for k in (0, 2):
        answer = functools.partial(
            pl.semaphore_signal, ready_sems.at[k + 1], inc=1, device_id=(targets[k],), device_id_type=mesh_id
        )
        pl.when(me + offsets[k] >= members)(answer)
    sends = []
    for k in range(4):
        size = PACKET if k < 2 else 24
        sends.append(
            pltpu.make_async_remote_copy(
                src_ref=outgoing.at[k, pl.ds(0, size)],
                dst_ref=incoming.at[k, pl.ds(0, size)],
                send_sem=send_sems.at[k],
                recv_sem=recv_sems.at[k],
                device_id=(targets[k],),
                device_id_type=mesh_id,
            )
        )
        if offsets[k] > 0:
            sends[k].start()
        else:
            pl.when(me + offsets[k] >= 0)(sends[k].start)

    def send_late():
        for k in (1, 3):

            @pl.when(me + offsets[k] < 0)
            def _(k=k):
                pl.semaphore_wait(ready_sems.at[k], 1)
                sends[k].start()

    copies[6].wait()
    copies[8].wait()
    for t in range(ROWS):
        index = neighbors_v[:, 128 * t : 128 * t + 128]
        neighbors_t[8 * t : 8 * t + 6, :] = index
        half = (index >> 12) & 1
        column_t[8 * t : 8 * t + 6, :] = ((index & 127) + 128 * half + 256 * (index >> 13)).astype(FLOAT)
        row_t[8 * t : 8 * t + 6, :] = (index >> 7) & 31
        weights_t[8 * t : 8 * t + 6, :] = weights_v[:, 128 * t : 128 * t + 128]
    for c in range(3):
        for half in range(2):
            for q in range(2):
                part = jnp.concatenate(
                    [gradient_t[pl.ds(4 * (32 * half + 16 * q + 8 * u) + c, 8, stride=4), :] for u in range(2)], axis=0
                )
                for s in range(3):
                    piece = part.astype(jnp.bfloat16)
                    at = 96 * s + 32 * c + 16 * q
                    table[at : at + 16, 128 * half : 128 * half + 128] = piece
                    part = part - piece.astype(FLOAT)
    steps[...] = lax.broadcasted_iota(jnp.int32, (256, 128), 0).astype(FLOAT).astype(jnp.bfloat16)
    sublane = lax.broadcasted_iota(jnp.int32, (8, 128), 0)
    one, zero = jnp.ones((), jnp.bfloat16), jnp.zeros((), jnp.bfloat16)

    def wide(ref, at):
        return jnp.broadcast_to(ref[pl.ds(at, 1), :], (8, 128))

    def own_block(block):
        for p in range(4):
            sums = [jnp.zeros((8, 128), FLOAT) for _ in range(2)]
            rows = [8 * block + 2 * p + e for e in range(2)]
            for m in range(6):
                hot = []
                for e in range(2):
                    column = jnp.broadcast_to(column_t[pl.ds(8 * rows[e] + m, 1), :], (16, 128))
                    column = jnp.concatenate([column.astype(jnp.bfloat16)] * 16, axis=0)
                    hot.append(jnp.where(column == steps[...], one, zero))
                hot = jnp.concatenate(hot, axis=1)
                got = jnp.dot(table[...], hot, preferred_element_type=FLOAT)
                got = got[0:96] + got[96:192] + got[192:288]
                for e in range(2):
                    row = wide(row_t, 8 * rows[e] + m)
                    hits = [row == sublane + 8 * g for g in range(4)]
                    square = None
                    for c in range(3):
                        value = jnp.zeros((8, 128), FLOAT)
                        for g in range(4):
                            at = 32 * c + 8 * g
                            value = jnp.where(hits[g], got[at : at + 8, 128 * e : 128 * e + 128], value)
                        jump = wide(gradient_t, 4 * rows[e] + c) - value
                        square = jump * jump if square is None else square + jump * jump
                    here = jnp.logical_and((row & 7) == sublane, wide(column_t, 8 * rows[e] + m) < 256.0)
                    sums[e] = sums[e] + jnp.where(here, wide(weights_t, 8 * rows[e] + m) * square, 0.0)
            for e in range(2):
                own_sum[pl.ds(rows[e], 1), :] = jnp.sum(sums[e], axis=0, keepdims=True)

    def ghost_unit(unit, odd):
        block = unit // 6
        m = unit - 6 * block
        base = pl.multiple_of(block * 64, 64)
        index = neighbors_t[pl.ds(base + m, 8, stride=8), :]
        lanes, rows = index & 127, index >> 7
        totals = [jnp.zeros((8, 128), FLOAT) for _ in range(3)]
        for k in (odd, 2 + odd):
            for s in range(8):
                hit = rows == ROWS + 8 * k + s
                for c in range(3):
                    got = lookup(incoming[k, 8 * c + s : 8 * c + s + 1, :], lanes)
                    totals[c] = jnp.where(hit, got, totals[c])
        square = None
        for c in range(3):
            jump = gradient_t[pl.ds(pl.multiple_of(block * 32, 32) + c, 8, stride=4), :] - totals[c]
            square = jump * jump if square is None else square + jump * jump
        here = jnp.logical_and(rows >= ROWS, ((rows >> 3) & 1) == odd)
        terms[odd, unit] = jnp.where(here, weights_t[pl.ds(base + m, 8, stride=8), :] * square, 0.0)

    def alone(block, carry):
        own_block(block)
        return carry

    def beside(odd, first_block, step, carry):
        if odd:
            pl.when(step == 2)(send_late)
        for v in range(16):
            ghost_unit(16 * step + v, odd)
        own_block(first_block + step)
        return carry

    lax.fori_loop(0, 2, alone, 0)
    sends[1].wait_recv()
    sends[3].wait_recv()
    lax.fori_loop(0, 3, functools.partial(beside, 1, 2), 0)
    sends[0].wait_recv()
    sends[2].wait_recv()
    lax.fori_loop(0, 3, functools.partial(beside, 0, 5), 0)
    for block in range(BLOCKS):
        total = own_sum[8 * block : 8 * block + 8, :]
        for m in range(6):
            total = total + (terms[0, 6 * block + m] + terms[1, 6 * block + m])
        indicator[8 * block : 8 * block + 8, :] = total

    for f in range(FIELDS):
        at = 24 + MARGIN_ROWS * f
        window[f, OWN_AT - MARGIN_ROWS : OWN_AT, :] = incoming[0, at : at + MARGIN_ROWS, :]
        right = OWN_AT + ROWS
        window[f, right : right + 8, :] = jnp.zeros((8, 128), FLOAT)
        window[f, right + 8 : right + 16, :] = jnp.zeros((8, 128), FLOAT)
        window[f, right : right + MARGIN_ROWS, :] = incoming[1, at : at + MARGIN_ROWS, :]
    copies[7].wait()
    owners = lax.broadcasted_iota(jnp.int32, (1, 128), 1)
    held = counts_v[...]
    begin = jnp.sum(jnp.where(owners < me, held, 0))
    count = jnp.sum(jnp.where(owners == me, held, 0))
    count = jnp.minimum(count, members * ELEMENTS - begin)
    start = jnp.clip(begin - me * ELEMENTS + MARGIN, 0, 2 * MARGIN)
    first, turn = start // 128, start % 128
    first = first + OWN_AT - MARGIN_ROWS
    lane = lax.broadcasted_iota(jnp.int32, (8, 128), 1)
    slot = lax.broadcasted_iota(jnp.int32, (8, 128), 0) * 128 + lane
    turned = (lane + turn) & 127
    low = lane < 128 - turn
    for f in range(FIELDS):
        for b in range(OUT_ROWS // 8):
            here = window[f, pl.ds(first + 8 * b, 8), :]
            there = window[f, pl.ds(first + 8 * b + 1, 8), :]
            both = [jnp.take_along_axis(v, turned, axis=1, mode="promise_in_bounds") for v in (here, there)]
            value = jnp.where(low, both[0], both[1])
            if f in (0, 5, 6, 7):
                value = jnp.where(slot + 1024 * b < count, value, 0.0)
            shifted[f, 8 * b : 8 * b + 8, :] = value

    child = lax.broadcasted_iota(jnp.int32, (8, 128), 0)
    signs = [(2 * ((child >> c) & 1) - 1).astype(FLOAT) for c in range(3)]
    eldest = child == 0
    for t in range(OUT_ROWS):
        row = [jnp.broadcast_to(shifted[f, t : t + 1, :], (8, 128)) for f in range(FIELDS)]
        slope = signs[0] * row[1] + signs[1] * row[2] + signs[2] * row[3]
        refined = row[7] > 0.0
        kept = jnp.logical_or(refined, eldest)
        at = slice(128 * t, 128 * t + 128)
        moved = jnp.where(refined, row[0] + row[4] * slope, row[0])
        children[0, :, at] = jnp.where(kept, moved, 0.0)
        children[1, :, at] = jnp.where(kept, row[5], 0.0)
        children[2, :, at] = jnp.where(kept, row[6], 0.0)
    for send in sends:
        send.wait_send()


def local(
    members,
    density,
    gradient,
    elem_size,
    history,
    refine_flags,
    face_neighbor,
    face_weight,
    ghost_send,
    new_counts,
):
    vmem = pltpu.VMEM
    flat = (ROWS, 128)
    operands = (
        density.reshape(flat),
        gradient,
        elem_size.reshape(flat),
        history,
        refine_flags.reshape(flat),
        face_neighbor,
        face_weight,
        ghost_send,
        new_counts.reshape(1, 128),
    )
    operands = [pltpu.with_memory_space_constraint(x, pltpu.HBM) for x in operands]
    indicator, children = pl.pallas_call(
        functools.partial(kernel, members),
        out_shape=(
            jax.ShapeDtypeStruct(flat, FLOAT),
            jax.ShapeDtypeStruct((3, 8, CAPACITY), FLOAT),
        ),
        in_specs=[pl.BlockSpec(memory_space=pltpu.HBM)] * 9,
        out_specs=(pl.BlockSpec(memory_space=vmem),) * 2,
        scratch_shapes=[
            vmem(flat, FLOAT),
            vmem((3, ELEMENTS), FLOAT),
            vmem(flat, FLOAT),
            vmem((2, ELEMENTS), FLOAT),
            vmem(flat, jnp.int32),
            vmem((6, ELEMENTS), jnp.int32),
            vmem((6, ELEMENTS), FLOAT),
            vmem((4, GHOST), jnp.int32),
            vmem((1, 128), jnp.int32),
            vmem((4 * ROWS, 128), FLOAT),
            vmem((2 * ROWS, 128), FLOAT),
            vmem((8 * ROWS, 128), jnp.int32),
            vmem((8 * ROWS, 128), FLOAT),
            vmem((32, 128), jnp.int32),
            vmem((8 * ROWS, 128), FLOAT),
            vmem((8 * ROWS, 128), jnp.int32),
            vmem((288, 256), jnp.bfloat16),
            vmem((256, 128), jnp.bfloat16),
            vmem(flat, FLOAT),
            vmem((2, 6 * BLOCKS, 8, 128), FLOAT),
            vmem((FIELDS, WINDOW, 128), FLOAT),
            vmem((FIELDS, OUT_ROWS, 128), FLOAT),
            vmem((4, PACKET, 128), FLOAT),
            vmem((4, PACKET, 128), FLOAT),
            pltpu.SemaphoreType.DMA((9,)),
            pltpu.SemaphoreType.DMA((4,)),
            pltpu.SemaphoreType.DMA((4,)),
            pltpu.SemaphoreType.REGULAR((4,)),
        ],
        compiler_params=pltpu.CompilerParams(
            collective_id=0, has_side_effects=True, vmem_limit_bytes=32 * 1024 * 1024
        ),
    )(*operands)
    return indicator.reshape(ELEMENTS), children


def solution(mesh):
    placed = (
        P("dom"),
        P(None, "dom"),
        P("dom"),
        P(None, "dom"),
        P("dom"),
        P(None, "dom"),
        P(None, "dom"),
        P("dom", None),
        P(),
    )
    return jax.shard_map(
        functools.partial(local, mesh.shape["dom"]),
        mesh=mesh,
        in_specs=placed,
        out_specs=(P("dom"), P(None, None, "dom")),
        check_vma=False,
    )
```

```python
import functools

import jax
import jax.numpy as jnp
from jax import lax
from jax.experimental import pallas as pl
from jax.experimental.pallas import tpu as pltpu
from jax.sharding import PartitionSpec as P

ELEMENTS = 8192
ROWS = ELEMENTS // 128
BLOCKS = ROWS // 8
GHOST = 1024
MARGIN = 512
MARGIN_ROWS = MARGIN // 128
CAPACITY = ELEMENTS + 2 * MARGIN
OUT_ROWS = CAPACITY // 128
FIELDS = 8
OWN_AT = 8
WINDOW = 96
FLOAT = jnp.float32
HOT = 24
PART = 80


def lookup(row, lanes):
    wide = jnp.broadcast_to(row, (8, 128))
    return jnp.take_along_axis(wide, lanes, axis=1, mode="promise_in_bounds")


def kernel(
    members,
    density,
    gradient,
    elem_size,
    history,
    flags,
    neighbors,
    weights,
    ghost_send,
    counts,
    indicator,
    children,
    density_v,
    gradient_v,
    size_v,
    history_v,
    flags_v,
    neighbors_v,
    weights_v,
    ghost_v,
    counts_v,
    gradient_t,
    history_t,
    neighbors_t,
    weights_t,
    ghost_t,
    column_t,
    row_t,
    table,
    steps,
    own_sum,
    terms,
    window,
    shifted,
    outgoing,
    incoming,
    edges,
    beyond,
    local_sems,
    send_sems,
    recv_sems,
    ready_sems,
):
    me = lax.axis_index("dom")
    far = members // 8
    targets = [lax.rem(me + o + members, members) for o in (1, -1, far, -far)]

    pairs = (
        (gradient, gradient_v),
        (ghost_send, ghost_v),
        (density, density_v),
        (elem_size, size_v),
        (history, history_v),
        (flags, flags_v),
        (neighbors, neighbors_v),
        (counts, counts_v),
        (weights, weights_v),
    )
    copies = [
        pltpu.make_async_copy(source, target, local_sems.at[i])
        for i, (source, target) in enumerate(pairs)
    ]
    for copy in copies[:2]:
        copy.start()

    mesh_id = pl.DeviceIdType.MESH
    barrier = pltpu.get_barrier_semaphore()

    def signal(semaphore, k):
        pl.semaphore_signal(semaphore, inc=1, device_id=(targets[k],), device_id_type=mesh_id)

    last_line = members - far
    pl.when(me < members - 1)(lambda: signal(barrier, 0))
    signal(barrier, 1)
    pl.when(me < last_line)(lambda: signal(barrier, 2))
    pl.when(me < far)(lambda: signal(barrier, 3))
    for copy in copies[2:]:
        copy.start()

    copies[0].wait()
    copies[1].wait()
    for t in range(8):
        ghost_t[4 * t : 4 * t + 4, :] = ghost_v[:, 128 * t : 128 * t + 128]
    for k in range(4):
        index = ghost_t[pl.ds(k, 8, stride=4), :]
        lanes, rows = index & 127, index >> 7
        totals = [jnp.zeros((8, 128), FLOAT) for _ in range(3)]
        for r in range(ROWS):
            hit = rows == r
            for c in range(3):
                got = lookup(gradient_v[c : c + 1, 128 * r : 128 * r + 128], lanes)
                totals[c] = jnp.where(hit, got, totals[c])
        for c in range(3):
            outgoing[k, 8 * c : 8 * c + 8, :] = totals[c]

    for t in range(ROWS):
        gradient_t[4 * t : 4 * t + 3, :] = gradient_v[:, 128 * t : 128 * t + 128]
    for i in (2, 3, 4, 5):
        copies[i].wait()
    for t in range(ROWS):
        history_t[2 * t : 2 * t + 2, :] = history_v[:, 128 * t : 128 * t + 128]
    for b in range(BLOCKS):
        own = slice(8 * b, 8 * b + 8)
        at = slice(OWN_AT + 8 * b, OWN_AT + 8 * b + 8)
        window[0, at, :] = density_v[own, :]
        for c in range(3):
            window[1 + c, at, :] = gradient_t[pl.ds(32 * b + c, 8, stride=4), :]
        window[4, at, :] = 0.25 * size_v[own, :]
        for c in range(2):
            window[5 + c, at, :] = history_t[pl.ds(16 * b + c, 8, stride=2), :]
        window[7, at, :] = flags_v[own, :].astype(FLOAT)
    for f in range(FIELDS):
        at = MARGIN_ROWS * f
        last = OWN_AT + ROWS - MARGIN_ROWS
        edges[0, at : at + MARGIN_ROWS, :] = window[f, last : last + MARGIN_ROWS, :]
        edges[1, at : at + MARGIN_ROWS, :] = window[f, OWN_AT : OWN_AT + MARGIN_ROWS, :]

    def packet(k, target):
        return pltpu.make_async_remote_copy(
            src_ref=outgoing.at[k],
            dst_ref=incoming.at[k],
            send_sem=send_sems.at[k],
            recv_sem=recv_sems.at[k],
            device_id=(target,),
            device_id_type=mesh_id,
        )

    margins = [
        pltpu.make_async_remote_copy(
            src_ref=edges.at[k],
            dst_ref=beyond.at[k],
            send_sem=send_sems.at[4 + k],
            recv_sem=recv_sems.at[4 + k],
            device_id=(targets[k],),
            device_id_type=mesh_id,
        )
        for k in range(2)
    ]
    sends = [packet(k, targets[k]) for k in range(4)]

    heard = 3 - (me < far).astype(jnp.int32) - (me == 0).astype(jnp.int32)
    pl.semaphore_wait(barrier, heard + (me >= last_line).astype(jnp.int32))
    pl.when(me >= far)(lambda: signal(ready_sems.at[2], 3))
    pl.when(me >= last_line)(lambda: signal(ready_sems.at[3], 2))
    pl.when(me == members - 1)(lambda: signal(ready_sems.at[1], 0))
    sends[0].start()
    pl.when(me > 0)(sends[1].start)
    pl.when(me >= far)(sends[3].start)
    pl.when(me >= last_line)(sends[2].start)
    margins[0].start()
    pl.when(me > 0)(margins[1].start)

    def send_late(k, where):
        @pl.when(where)
        def _():
            pl.semaphore_wait(ready_sems.at[k], 1)
            sends[k].start()
            if k == 1:
                margins[1].start()

    start, end = me == 0, me == members - 1
    order = [
        jnp.where(start, 1, 0),
        jnp.where(start, 3, jnp.where(end, 2, 1)),
        jnp.where(start, 2, jnp.where((me < far) | end, 3, 2)),
        jnp.where(start, 0, jnp.where(end, 1, jnp.where(me < far, 2, 3))),
    ]

    def arrived(k):
        packet(k, targets[0]).wait_recv()

    copies[6].wait()
    copies[8].wait()
    for t in range(ROWS):
        index = neighbors_v[:, 128 * t : 128 * t + 128]
        neighbors_t[8 * t : 8 * t + 6, :] = index
        half = (index >> 12) & 1
        row = (index >> 7) & 31
        elsewhere = jnp.where(jnp.logical_or(index >= ELEMENTS, row >= HOT), 256, 0)
        column_t[8 * t : 8 * t + 6, :] = ((index & 127) + 128 * half + elsewhere).astype(FLOAT)
        row_t[8 * t : 8 * t + 6, :] = row
        weights_t[8 * t : 8 * t + 6, :] = weights_v[:, 128 * t : 128 * t + 128]
    for half in range(2):
        groups = [
            gradient_t[pl.ds(4 * (32 * half + 8 * q) + c, 8, stride=4), :]
            for c in range(3)
            for q in range(HOT // 8)
        ] + [jnp.zeros((8, 128), FLOAT)]
        for g in range(0, len(groups), 2):
            part = jnp.concatenate(groups[g : g + 2], axis=0)
            for s in range(3):
                piece = part.astype(jnp.bfloat16)
                at = PART * s + 8 * g
                table[at : at + 16, 128 * half : 128 * half + 128] = piece
                part = part - piece.astype(FLOAT)
    steps[...] = lax.broadcasted_iota(jnp.int32, (256, 128), 0).astype(FLOAT).astype(jnp.bfloat16)
    sublane = lax.broadcasted_iota(jnp.int32, (8, 128), 0)
    one, zero = jnp.ones((), jnp.bfloat16), jnp.zeros((), jnp.bfloat16)

    def wide(ref, at):
        return jnp.broadcast_to(ref[pl.ds(at, 1), :], (8, 128))

    def own_pairs(first, number):
        for p in range(number):
            sums = [jnp.zeros((8, 128), FLOAT) for _ in range(2)]
            rows = [2 * (first + p) + e for e in range(2)]
            for m in range(6):
                hot = []
                for e in range(2):
                    column = jnp.broadcast_to(column_t[pl.ds(8 * rows[e] + m, 1), :], (16, 128))
                    column = jnp.concatenate([column.astype(jnp.bfloat16)] * 16, axis=0)
                    hot.append(jnp.where(column == steps[...], one, zero))
                hot = jnp.concatenate(hot, axis=1)
                got = jnp.dot(table[...], hot, preferred_element_type=FLOAT)
                got = got[0 : 3 * HOT] + got[PART : PART + 3 * HOT] + got[2 * PART : 2 * PART + 3 * HOT]
                for e in range(2):
                    row = wide(row_t, 8 * rows[e] + m)
                    hits = [row == sublane + 8 * g for g in range(HOT // 8)]
                    square = None
                    for c in range(3):
                        value = jnp.zeros((8, 128), FLOAT)
                        for g in range(HOT // 8):
                            at = HOT * c + 8 * g
                            value = jnp.where(hits[g], got[at : at + 8, 128 * e : 128 * e + 128], value)
                        jump = wide(gradient_t, 4 * rows[e] + c) - value
                        square = jump * jump if square is None else square + jump * jump
                    here = jnp.logical_and((row & 7) == sublane, wide(column_t, 8 * rows[e] + m) < 256.0)
                    sums[e] = sums[e] + jnp.where(here, wide(weights_t, 8 * rows[e] + m) * square, 0.0)
            for e in range(2):
                own_sum[pl.ds(rows[e], 1), :] = jnp.sum(sums[e], axis=0, keepdims=True)

    def unit_terms(unit, group, found_rows, inside):
        block = unit // 6
        m = unit - 6 * block
        base = pl.multiple_of(block * 64, 64)
        index = neighbors_t[pl.ds(base + m, 8, stride=8), :]
        lanes, rows = index & 127, index >> 7
        totals = [jnp.zeros((8, 128), FLOAT) for _ in range(3)]
        for row, entries in found_rows:
            hit = rows == row
            for c in range(3):
                totals[c] = jnp.where(hit, lookup(entries(c), lanes), totals[c])
        square = None
        for c in range(3):
            jump = gradient_t[pl.ds(pl.multiple_of(block * 32, 32) + c, 8, stride=4), :] - totals[c]
            square = jump * jump if square is None else square + jump * jump
        weight = weights_t[pl.ds(base + m, 8, stride=8), :]
        terms[group, unit] = jnp.where(inside(rows), weight * square, 0.0)

    def rest_unit(unit):
        found_rows = [
            (r, lambda c, r=r: gradient_v[c : c + 1, 128 * r : 128 * r + 128])
            for h in range(2)
            for r in range(32 * h + HOT, 32 * h + 32)
        ]
        unit_terms(unit, 3, found_rows, lambda rows: jnp.logical_and(rows < ROWS, (rows & 31) >= HOT))

    def ghost_unit(unit, group, sources):
        found_rows = [
            (ROWS + 8 * k + s, lambda c, k=k, s=s: incoming[k, 8 * c + s : 8 * c + s + 1, :])
            for k in sources
            for s in range(8)
        ]

        def inside(rows):
            return functools.reduce(jnp.logical_or, [(rows >> 3) == 8 + k for k in sources])

        unit_terms(unit, group, found_rows, inside)

    def rest(step, carry):
        for v in range(16):
            rest_unit(16 * step + v)
        own_pairs(4 * step, 4)
        return carry

    def pair(step, carry):
        send_late(2, (step == 1) & (me < last_line))
        for v in range(16):
            ghost_unit(16 * step + v, 0, order[:2])
        own_pairs(12 + 4 * step, 4)
        return carry

    lax.fori_loop(0, 3, rest, 0)
    arrived(order[0])
    arrived(order[1])
    lax.fori_loop(0, 3, pair, 0)
    send_late(3, me < far)
    arrived(order[2])
    for v in range(48):
        ghost_unit(v, 1, order[2:3])
    own_pairs(24, 4)
    send_late(1, start)
    arrived(order[3])
    for v in range(48):
        ghost_unit(v, 2, order[3:])
    own_pairs(28, 4)
    for block in range(BLOCKS):
        total = own_sum[8 * block : 8 * block + 8, :]
        for m in range(6):
            for group in range(4):
                total = total + terms[group, 6 * block + m]
        indicator[8 * block : 8 * block + 8, :] = total

    for margin in margins:
        margin.wait_recv()
    for f in range(FIELDS):
        at = MARGIN_ROWS * f
        window[f, OWN_AT - MARGIN_ROWS : OWN_AT, :] = beyond[0, at : at + MARGIN_ROWS, :]
        right = OWN_AT + ROWS
        window[f, right : right + 8, :] = jnp.zeros((8, 128), FLOAT)
        window[f, right + 8 : right + 16, :] = jnp.zeros((8, 128), FLOAT)
        window[f, right : right + MARGIN_ROWS, :] = beyond[1, at : at + MARGIN_ROWS, :]
    copies[7].wait()
    owners = lax.broadcasted_iota(jnp.int32, (1, 128), 1)
    held = counts_v[...]
    begin = jnp.sum(jnp.where(owners < me, held, 0))
    count = jnp.sum(jnp.where(owners == me, held, 0))
    count = jnp.minimum(count, members * ELEMENTS - begin)
    start = jnp.clip(begin - me * ELEMENTS + MARGIN, 0, 2 * MARGIN)
    first, turn = start // 128, start % 128
    first = first + OWN_AT - MARGIN_ROWS
    lane = lax.broadcasted_iota(jnp.int32, (8, 128), 1)
    slot = lax.broadcasted_iota(jnp.int32, (8, 128), 0) * 128 + lane
    turned = (lane + turn) & 127
    low = lane < 128 - turn
    for f in range(FIELDS):
        for b in range(OUT_ROWS // 8):
            here = window[f, pl.ds(first + 8 * b, 8), :]
            there = window[f, pl.ds(first + 8 * b + 1, 8), :]
            both = [jnp.take_along_axis(v, turned, axis=1, mode="promise_in_bounds") for v in (here, there)]
            value = jnp.where(low, both[0], both[1])
            if f in (0, 5, 6, 7):
                value = jnp.where(slot + 1024 * b < count, value, 0.0)
            shifted[f, 8 * b : 8 * b + 8, :] = value

    child = lax.broadcasted_iota(jnp.int32, (8, 128), 0)
    signs = [(2 * ((child >> c) & 1) - 1).astype(FLOAT) for c in range(3)]
    eldest = child == 0
    for t in range(OUT_ROWS):
        row = [jnp.broadcast_to(shifted[f, t : t + 1, :], (8, 128)) for f in range(FIELDS)]
        slope = signs[0] * row[1] + signs[1] * row[2] + signs[2] * row[3]
        refined = row[7] > 0.0
        kept = jnp.logical_or(refined, eldest)
        at = slice(128 * t, 128 * t + 128)
        moved = jnp.where(refined, row[0] + row[4] * slope, row[0])
        children[0, :, at] = jnp.where(kept, moved, 0.0)
        children[1, :, at] = jnp.where(kept, row[5], 0.0)
        children[2, :, at] = jnp.where(kept, row[6], 0.0)
    for send in sends + margins:
        send.wait_send()


def local(
    members,
    density,
    gradient,
    elem_size,
    history,
    refine_flags,
    face_neighbor,
    face_weight,
    ghost_send,
    new_counts,
):
    vmem = pltpu.VMEM
    flat = (ROWS, 128)
    operands = (
        density.reshape(flat),
        gradient,
        elem_size.reshape(flat),
        history,
        refine_flags.reshape(flat),
        face_neighbor,
        face_weight,
        ghost_send,
        new_counts.reshape(1, 128),
    )
    operands = [pltpu.with_memory_space_constraint(x, pltpu.HBM) for x in operands]
    indicator, children = pl.pallas_call(
        functools.partial(kernel, members),
        out_shape=(
            jax.ShapeDtypeStruct(flat, FLOAT),
            jax.ShapeDtypeStruct((3, 8, CAPACITY), FLOAT),
        ),
        in_specs=[pl.BlockSpec(memory_space=pltpu.HBM)] * 9,
        out_specs=(pl.BlockSpec(memory_space=vmem),) * 2,
        scratch_shapes=[
            vmem(flat, FLOAT),
            vmem((3, ELEMENTS), FLOAT),
            vmem(flat, FLOAT),
            vmem((2, ELEMENTS), FLOAT),
            vmem(flat, jnp.int32),
            vmem((6, ELEMENTS), jnp.int32),
            vmem((6, ELEMENTS), FLOAT),
            vmem((4, GHOST), jnp.int32),
            vmem((1, 128), jnp.int32),
            vmem((4 * ROWS, 128), FLOAT),
            vmem((2 * ROWS, 128), FLOAT),
            vmem((8 * ROWS, 128), jnp.int32),
            vmem((8 * ROWS, 128), FLOAT),
            vmem((32, 128), jnp.int32),
            vmem((8 * ROWS, 128), FLOAT),
            vmem((8 * ROWS, 128), jnp.int32),
            vmem((3 * PART, 256), jnp.bfloat16),
            vmem((256, 128), jnp.bfloat16),
            vmem(flat, FLOAT),
            vmem((4, 6 * BLOCKS, 8, 128), FLOAT),
            vmem((FIELDS, WINDOW, 128), FLOAT),
            vmem((FIELDS, OUT_ROWS, 128), FLOAT),
            vmem((4, 24, 128), FLOAT),
            vmem((4, 24, 128), FLOAT),
            vmem((2, FIELDS * MARGIN_ROWS, 128), FLOAT),
            vmem((2, FIELDS * MARGIN_ROWS, 128), FLOAT),
            pltpu.SemaphoreType.DMA((9,)),
            pltpu.SemaphoreType.DMA((6,)),
            pltpu.SemaphoreType.DMA((6,)),
            pltpu.SemaphoreType.REGULAR((4,)),
        ],
        compiler_params=pltpu.CompilerParams(
            collective_id=0, has_side_effects=True, vmem_limit_bytes=32 * 1024 * 1024
        ),
    )(*operands)
    return indicator.reshape(ELEMENTS), children


def solution(mesh):
    placed = (
        P("dom"),
        P(None, "dom"),
        P("dom"),
        P(None, "dom"),
        P("dom"),
        P(None, "dom"),
        P(None, "dom"),
        P("dom", None),
        P(),
    )
    return jax.shard_map(
        functools.partial(local, mesh.shape["dom"]),
        mesh=mesh,
        in_specs=placed,
        out_specs=(P("dom"), P(None, None, "dom")),
        check_vma=False,
    )
```

```python
import functools

import jax
import jax.numpy as jnp
from jax import lax
from jax.experimental import pallas as pl
from jax.experimental.pallas import tpu as pltpu
from jax.sharding import PartitionSpec as P

ELEMENTS = 8192
ROWS = ELEMENTS // 128
BLOCKS = ROWS // 8
GHOST = 1024
MARGIN = 512
MARGIN_ROWS = MARGIN // 128
CAPACITY = ELEMENTS + 2 * MARGIN
OUT_ROWS = CAPACITY // 128
CHUNK = 24
FIELDS = 8
OWN_AT = 8
WINDOW = 96
FLOAT = jnp.float32
HOT = 24
PART = 80


def lookup(row, lanes):
    wide = jnp.broadcast_to(row, (8, 128))
    return jnp.take_along_axis(wide, lanes, axis=1, mode="promise_in_bounds")


def kernel(
    members,
    density,
    gradient,
    elem_size,
    history,
    flags,
    neighbors,
    weights,
    ghost_send,
    counts,
    window,
    own_sum,
    terms,
    counts_out,
    density_v,
    gradient_v,
    size_v,
    history_v,
    flags_v,
    neighbors_v,
    weights_v,
    ghost_v,
    counts_v,
    gradient_t,
    history_t,
    neighbors_t,
    weights_t,
    ghost_t,
    column_t,
    row_t,
    table,
    steps,
    outgoing,
    incoming,
    edges,
    beyond,
    local_sems,
    send_sems,
    recv_sems,
    ready_sems,
):
    me = lax.axis_index("dom")
    far = members // 8
    targets = [lax.rem(me + o + members, members) for o in (1, -1, far, -far)]

    pairs = (
        (gradient, gradient_v),
        (ghost_send, ghost_v),
        (density, density_v),
        (elem_size, size_v),
        (history, history_v),
        (flags, flags_v),
        (neighbors, neighbors_v),
        (counts, counts_v),
        (weights, weights_v),
    )
    copies = [
        pltpu.make_async_copy(source, target, local_sems.at[i])
        for i, (source, target) in enumerate(pairs)
    ]
    for copy in copies[:2]:
        copy.start()

    mesh_id = pl.DeviceIdType.MESH
    barrier = pltpu.get_barrier_semaphore()

    def signal(semaphore, k):
        pl.semaphore_signal(semaphore, inc=1, device_id=(targets[k],), device_id_type=mesh_id)

    last_line = members - far
    pl.when(me < members - 1)(lambda: signal(barrier, 0))
    signal(barrier, 1)
    pl.when(me < last_line)(lambda: signal(barrier, 2))
    pl.when(me < far)(lambda: signal(barrier, 3))
    for copy in copies[2:]:
        copy.start()

    copies[0].wait()
    copies[1].wait()
    for t in range(8):
        ghost_t[4 * t : 4 * t + 4, :] = ghost_v[:, 128 * t : 128 * t + 128]
    for k in range(4):
        index = ghost_t[pl.ds(k, 8, stride=4), :]
        lanes, rows = index & 127, index >> 7
        totals = [jnp.zeros((8, 128), FLOAT) for _ in range(3)]
        for r in range(ROWS):
            hit = rows == r
            for c in range(3):
                got = lookup(gradient_v[c : c + 1, 128 * r : 128 * r + 128], lanes)
                totals[c] = jnp.where(hit, got, totals[c])
        for c in range(3):
            outgoing[k, 8 * c : 8 * c + 8, :] = totals[c]

    for t in range(ROWS):
        gradient_t[4 * t : 4 * t + 3, :] = gradient_v[:, 128 * t : 128 * t + 128]
    for i in (2, 3, 4, 5):
        copies[i].wait()
    for t in range(ROWS):
        history_t[2 * t : 2 * t + 2, :] = history_v[:, 128 * t : 128 * t + 128]
    for b in range(BLOCKS):
        own = slice(8 * b, 8 * b + 8)
        at = slice(OWN_AT + 8 * b, OWN_AT + 8 * b + 8)
        window[0, at, :] = density_v[own, :]
        for c in range(3):
            window[1 + c, at, :] = gradient_t[pl.ds(32 * b + c, 8, stride=4), :]
        window[4, at, :] = 0.25 * size_v[own, :]
        for c in range(2):
            window[5 + c, at, :] = history_t[pl.ds(16 * b + c, 8, stride=2), :]
        window[7, at, :] = flags_v[own, :].astype(FLOAT)
    for f in range(FIELDS):
        at = MARGIN_ROWS * f
        last = OWN_AT + ROWS - MARGIN_ROWS
        edges[0, at : at + MARGIN_ROWS, :] = window[f, last : last + MARGIN_ROWS, :]
        edges[1, at : at + MARGIN_ROWS, :] = window[f, OWN_AT : OWN_AT + MARGIN_ROWS, :]

    def packet(k, target):
        return pltpu.make_async_remote_copy(
            src_ref=outgoing.at[k],
            dst_ref=incoming.at[k],
            send_sem=send_sems.at[k],
            recv_sem=recv_sems.at[k],
            device_id=(target,),
            device_id_type=mesh_id,
        )

    margins = [
        pltpu.make_async_remote_copy(
            src_ref=edges.at[k],
            dst_ref=beyond.at[k],
            send_sem=send_sems.at[4 + k],
            recv_sem=recv_sems.at[4 + k],
            device_id=(targets[k],),
            device_id_type=mesh_id,
        )
        for k in range(2)
    ]
    sends = [packet(k, targets[k]) for k in range(4)]

    heard = 3 - (me < far).astype(jnp.int32) - (me == 0).astype(jnp.int32)
    pl.semaphore_wait(barrier, heard + (me >= last_line).astype(jnp.int32))
    pl.when(me >= far)(lambda: signal(ready_sems.at[2], 3))
    pl.when(me >= last_line)(lambda: signal(ready_sems.at[3], 2))
    pl.when(me == members - 1)(lambda: signal(ready_sems.at[1], 0))
    sends[0].start()
    pl.when(me > 0)(sends[1].start)
    pl.when(me >= far)(sends[3].start)
    pl.when(me >= last_line)(sends[2].start)
    margins[0].start()
    pl.when(me > 0)(margins[1].start)

    def send_late(k, where):
        @pl.when(where)
        def _():
            pl.semaphore_wait(ready_sems.at[k], 1)
            sends[k].start()
            if k == 1:
                margins[1].start()

    start, end = me == 0, me == members - 1
    order = [
        jnp.where(start, 1, 0),
        jnp.where(start, 3, jnp.where(end, 2, 1)),
        jnp.where(start, 2, jnp.where((me < far) | end, 3, 2)),
        jnp.where(start, 0, jnp.where(end, 1, jnp.where(me < far, 2, 3))),
    ]

    def arrived(k):
        packet(k, targets[0]).wait_recv()

    copies[6].wait()
    copies[8].wait()
    for t in range(ROWS):
        index = neighbors_v[:, 128 * t : 128 * t + 128]
        neighbors_t[8 * t : 8 * t + 6, :] = index
        half = (index >> 12) & 1
        row = (index >> 7) & 31
        elsewhere = jnp.where(jnp.logical_or(index >= ELEMENTS, row >= HOT), 256, 0)
        column_t[8 * t : 8 * t + 6, :] = ((index & 127) + 128 * half + elsewhere).astype(FLOAT)
        row_t[8 * t : 8 * t + 6, :] = row
        weights_t[8 * t : 8 * t + 6, :] = weights_v[:, 128 * t : 128 * t + 128]
    for half in range(2):
        groups = [
            gradient_t[pl.ds(4 * (32 * half + 8 * q) + c, 8, stride=4), :]
            for c in range(3)
            for q in range(HOT // 8)
        ] + [jnp.zeros((8, 128), FLOAT)]
        for g in range(0, len(groups), 2):
            part = jnp.concatenate(groups[g : g + 2], axis=0)
            for s in range(3):
                piece = part.astype(jnp.bfloat16)
                at = PART * s + 8 * g
                table[at : at + 16, 128 * half : 128 * half + 128] = piece
                part = part - piece.astype(FLOAT)
    steps[...] = lax.broadcasted_iota(jnp.int32, (256, 128), 0).astype(FLOAT).astype(jnp.bfloat16)
    sublane = lax.broadcasted_iota(jnp.int32, (8, 128), 0)
    one, zero = jnp.ones((), jnp.bfloat16), jnp.zeros((), jnp.bfloat16)

    def wide(ref, at):
        return jnp.broadcast_to(ref[pl.ds(at, 1), :], (8, 128))

    def own_pairs(first, number):
        for p in range(number):
            sums = [jnp.zeros((8, 128), FLOAT) for _ in range(2)]
            rows = [2 * (first + p) + e for e in range(2)]
            for m in range(6):
                hot = []
                for e in range(2):
                    column = jnp.broadcast_to(column_t[pl.ds(8 * rows[e] + m, 1), :], (16, 128))
                    column = jnp.concatenate([column.astype(jnp.bfloat16)] * 16, axis=0)
                    hot.append(jnp.where(column == steps[...], one, zero))
                hot = jnp.concatenate(hot, axis=1)
                got = jnp.dot(table[...], hot, preferred_element_type=FLOAT)
                got = got[0 : 3 * HOT] + got[PART : PART + 3 * HOT] + got[2 * PART : 2 * PART + 3 * HOT]
                for e in range(2):
                    row = wide(row_t, 8 * rows[e] + m)
                    hits = [row == sublane + 8 * g for g in range(HOT // 8)]
                    square = None
                    for c in range(3):
                        value = jnp.zeros((8, 128), FLOAT)
                        for g in range(HOT // 8):
                            at = HOT * c + 8 * g
                            value = jnp.where(hits[g], got[at : at + 8, 128 * e : 128 * e + 128], value)
                        jump = wide(gradient_t, 4 * rows[e] + c) - value
                        square = jump * jump if square is None else square + jump * jump
                    here = jnp.logical_and((row & 7) == sublane, wide(column_t, 8 * rows[e] + m) < 256.0)
                    sums[e] = sums[e] + jnp.where(here, wide(weights_t, 8 * rows[e] + m) * square, 0.0)
            for e in range(2):
                own_sum[pl.ds(rows[e], 1), :] = jnp.sum(sums[e], axis=0, keepdims=True)

    def unit_terms(unit, group, found_rows, inside):
        block = unit // 6
        m = unit - 6 * block
        base = pl.multiple_of(block * 64, 64)
        index = neighbors_t[pl.ds(base + m, 8, stride=8), :]
        lanes, rows = index & 127, index >> 7
        totals = [jnp.zeros((8, 128), FLOAT) for _ in range(3)]
        for row, entries in found_rows:
            hit = rows == row
            for c in range(3):
                totals[c] = jnp.where(hit, lookup(entries(c), lanes), totals[c])
        square = None
        for c in range(3):
            jump = gradient_t[pl.ds(pl.multiple_of(block * 32, 32) + c, 8, stride=4), :] - totals[c]
            square = jump * jump if square is None else square + jump * jump
        weight = weights_t[pl.ds(base + m, 8, stride=8), :]
        terms[group, unit] = jnp.where(inside(rows), weight * square, 0.0)

    def rest_unit(unit):
        found_rows = [
            (r, lambda c, r=r: gradient_v[c : c + 1, 128 * r : 128 * r + 128])
            for h in range(2)
            for r in range(32 * h + HOT, 32 * h + 32)
        ]
        unit_terms(unit, 3, found_rows, lambda rows: jnp.logical_and(rows < ROWS, (rows & 31) >= HOT))

    def ghost_unit(unit, group, sources):
        found_rows = [
            (ROWS + 8 * k + s, lambda c, k=k, s=s: incoming[k, 8 * c + s : 8 * c + s + 1, :])
            for k in sources
            for s in range(8)
        ]

        def inside(rows):
            return functools.reduce(jnp.logical_or, [(rows >> 3) == 8 + k for k in sources])

        unit_terms(unit, group, found_rows, inside)

    def rest(step, carry):
        for v in range(16):
            rest_unit(16 * step + v)
        own_pairs(4 * step, 4)
        return carry

    def pair(step, carry):
        send_late(2, (step == 1) & (me < last_line))
        for v in range(16):
            ghost_unit(16 * step + v, 0, order[:2])
        own_pairs(12 + 4 * step, 4)
        return carry

    lax.fori_loop(0, 3, rest, 0)
    arrived(order[0])
    arrived(order[1])
    lax.fori_loop(0, 3, pair, 0)
    send_late(3, me < far)
    arrived(order[2])
    for v in range(48):
        ghost_unit(v, 1, order[2:3])
    own_pairs(24, 4)
    send_late(1, start)
    arrived(order[3])
    for v in range(48):
        ghost_unit(v, 2, order[3:])
    own_pairs(28, 4)
    for margin in margins:
        margin.wait_recv()
    for f in range(FIELDS):
        at = MARGIN_ROWS * f
        window[f, OWN_AT - MARGIN_ROWS : OWN_AT, :] = beyond[0, at : at + MARGIN_ROWS, :]
        right = OWN_AT + ROWS
        window[f, right : right + 8, :] = jnp.zeros((8, 128), FLOAT)
        window[f, right + 8 : right + 16, :] = jnp.zeros((8, 128), FLOAT)
        window[f, right : right + MARGIN_ROWS, :] = beyond[1, at : at + MARGIN_ROWS, :]
    copies[7].wait()
    counts_out[...] = counts_v[...]
    for send in sends + margins:
        send.wait_send()


def finish(members, window, own_sum, terms, counts, indicator, children, shifted, indicator_v, children_v, sems):
    me = lax.axis_index("dom")
    owners = lax.broadcasted_iota(jnp.int32, (1, 128), 1)
    held = counts[...]
    begin = jnp.sum(jnp.where(owners < me, held, 0))
    count = jnp.sum(jnp.where(owners == me, held, 0))
    count = jnp.minimum(count, members * ELEMENTS - begin)
    start = jnp.clip(begin - me * ELEMENTS + MARGIN, 0, 2 * MARGIN)
    first, turn = start // 128, start % 128
    first = first + OWN_AT - MARGIN_ROWS
    lane = lax.broadcasted_iota(jnp.int32, (8, 128), 1)
    slot = lax.broadcasted_iota(jnp.int32, (8, 128), 0) * 128 + lane
    turned = (lane + turn) & 127
    low = lane < 128 - turn
    for f in range(FIELDS):
        for b in range(OUT_ROWS // 8):
            here = window[f, pl.ds(first + 8 * b, 8), :]
            there = window[f, pl.ds(first + 8 * b + 1, 8), :]
            both = [jnp.take_along_axis(v, turned, axis=1, mode="promise_in_bounds") for v in (here, there)]
            value = jnp.where(low, both[0], both[1])
            if f in (0, 5, 6, 7):
                value = jnp.where(slot + 1024 * b < count, value, 0.0)
            shifted[f, 8 * b : 8 * b + 8, :] = value

    child = lax.broadcasted_iota(jnp.int32, (8, 128), 0)
    signs = [(2 * ((child >> c) & 1) - 1).astype(FLOAT) for c in range(3)]
    eldest = child == 0
    copies = []
    for t in range(OUT_ROWS):
        row = [jnp.broadcast_to(shifted[f, t : t + 1, :], (8, 128)) for f in range(FIELDS)]
        slope = signs[0] * row[1] + signs[1] * row[2] + signs[2] * row[3]
        refined = row[7] > 0.0
        kept = jnp.logical_or(refined, eldest)
        at = slice(128 * t, 128 * t + 128)
        moved = jnp.where(refined, row[0] + row[4] * slope, row[0])
        children_v[0, :, at] = jnp.where(kept, moved, 0.0)
        children_v[1, :, at] = jnp.where(kept, row[5], 0.0)
        children_v[2, :, at] = jnp.where(kept, row[6], 0.0)
        if (t + 1) % CHUNK == 0:
            part = pl.ds(128 * (t + 1 - CHUNK), 128 * CHUNK)
            out = pltpu.make_async_copy(children_v.at[:, :, part], children.at[:, :, part], sems.at[t // CHUNK])
            out.start()
            copies.append(out)
    for block in range(BLOCKS):
        total = own_sum[8 * block : 8 * block + 8, :]
        for m in range(6):
            for group in range(4):
                total = total + terms[group, 6 * block + m]
        indicator_v[8 * block : 8 * block + 8, :] = total
    out = pltpu.make_async_copy(indicator_v, indicator, sems.at[OUT_ROWS // CHUNK])
    out.start()
    for copy in copies + [out]:
        copy.wait()


def local(
    members,
    density,
    gradient,
    elem_size,
    history,
    refine_flags,
    face_neighbor,
    face_weight,
    ghost_send,
    new_counts,
):
    vmem = pltpu.VMEM
    flat = (ROWS, 128)
    operands = (
        density.reshape(flat),
        gradient,
        elem_size.reshape(flat),
        history,
        refine_flags.reshape(flat),
        face_neighbor,
        face_weight,
        ghost_send,
        new_counts.reshape(1, 128),
    )
    operands = [pltpu.with_memory_space_constraint(x, pltpu.HBM) for x in operands]
    handed = pl.pallas_call(
        functools.partial(kernel, members),
        out_shape=(
            vmem((FIELDS, WINDOW, 128), FLOAT),
            vmem(flat, FLOAT),
            vmem((4, 6 * BLOCKS, 8, 128), FLOAT),
            vmem((1, 128), jnp.int32),
        ),
        in_specs=[pl.BlockSpec(memory_space=pltpu.HBM)] * 9,
        out_specs=(pl.BlockSpec(memory_space=vmem),) * 4,
        scratch_shapes=[
            vmem(flat, FLOAT),
            vmem((3, ELEMENTS), FLOAT),
            vmem(flat, FLOAT),
            vmem((2, ELEMENTS), FLOAT),
            vmem(flat, jnp.int32),
            vmem((6, ELEMENTS), jnp.int32),
            vmem((6, ELEMENTS), FLOAT),
            vmem((4, GHOST), jnp.int32),
            vmem((1, 128), jnp.int32),
            vmem((4 * ROWS, 128), FLOAT),
            vmem((2 * ROWS, 128), FLOAT),
            vmem((8 * ROWS, 128), jnp.int32),
            vmem((8 * ROWS, 128), FLOAT),
            vmem((32, 128), jnp.int32),
            vmem((8 * ROWS, 128), FLOAT),
            vmem((8 * ROWS, 128), jnp.int32),
            vmem((3 * PART, 256), jnp.bfloat16),
            vmem((256, 128), jnp.bfloat16),
            vmem((4, 24, 128), FLOAT),
            vmem((4, 24, 128), FLOAT),
            vmem((2, FIELDS * MARGIN_ROWS, 128), FLOAT),
            vmem((2, FIELDS * MARGIN_ROWS, 128), FLOAT),
            pltpu.SemaphoreType.DMA((9,)),
            pltpu.SemaphoreType.DMA((6,)),
            pltpu.SemaphoreType.DMA((6,)),
            pltpu.SemaphoreType.REGULAR((4,)),
        ],
        compiler_params=pltpu.CompilerParams(
            collective_id=0, has_side_effects=True, vmem_limit_bytes=32 * 1024 * 1024
        ),
    )(*operands)
    handed = [pltpu.with_memory_space_constraint(x, vmem) for x in handed]
    indicator, children = pl.pallas_call(
        functools.partial(finish, members),
        out_shape=(pltpu.HBM(flat, FLOAT), pltpu.HBM((3, 8, CAPACITY), FLOAT)),
        in_specs=[pl.BlockSpec(memory_space=vmem)] * 4,
        out_specs=(pl.BlockSpec(memory_space=pltpu.HBM),) * 2,
        scratch_shapes=[
            vmem((FIELDS, OUT_ROWS, 128), FLOAT),
            vmem(flat, FLOAT),
            vmem((3, 8, CAPACITY), FLOAT),
            pltpu.SemaphoreType.DMA((OUT_ROWS // CHUNK + 1,)),
        ],
        compiler_params=pltpu.CompilerParams(vmem_limit_bytes=8 * 1024 * 1024),
    )(*handed)
    return indicator.reshape(ELEMENTS), children


def solution(mesh):
    placed = (
        P("dom"),
        P(None, "dom"),
        P("dom"),
        P(None, "dom"),
        P("dom"),
        P(None, "dom"),
        P(None, "dom"),
        P("dom", None),
        P(),
    )
    return jax.shard_map(
        functools.partial(local, mesh.shape["dom"]),
        mesh=mesh,
        in_specs=placed,
        out_specs=(P("dom"), P(None, None, "dom")),
        check_vma=False,
    )
```

```python
import functools

import jax
import jax.numpy as jnp
from jax import lax
from jax.experimental import pallas as pl
from jax.experimental.pallas import tpu as pltpu
from jax.sharding import PartitionSpec as P

ELEMENTS = 8192
ROWS = ELEMENTS // 128
BLOCKS = ROWS // 8
GHOST = 1024
MARGIN = 512
MARGIN_ROWS = MARGIN // 128
CAPACITY = ELEMENTS + 2 * MARGIN
OUT_ROWS = CAPACITY // 128
CHUNK = 24
FIELDS = 8
OWN_AT = 8
WINDOW = 96
FLOAT = jnp.float32
HOT = 24
PART = 80


def lookup(row, lanes):
    wide = jnp.broadcast_to(row, (8, 128))
    return jnp.take_along_axis(wide, lanes, axis=1, mode="promise_in_bounds")


def kernel(
    members,
    density,
    gradient,
    elem_size,
    history,
    flags,
    neighbors,
    weights,
    ghost_send,
    counts,
    window,
    own_sum,
    terms,
    counts_out,
    density_v,
    gradient_v,
    size_v,
    history_v,
    flags_v,
    neighbors_v,
    weights_v,
    ghost_v,
    counts_v,
    gradient_t,
    history_t,
    neighbors_t,
    weights_t,
    ghost_t,
    column_t,
    row_t,
    table,
    steps,
    outgoing,
    incoming,
    edges,
    beyond,
    local_sems,
    send_sems,
    recv_sems,
    ready_sems,
):
    me = lax.axis_index("dom")
    far = members // 8
    targets = [lax.rem(me + o + members, members) for o in (1, -1, far, -far)]

    pairs = (
        (gradient, gradient_v),
        (ghost_send, ghost_v),
        (density, density_v),
        (elem_size, size_v),
        (history, history_v),
        (flags, flags_v),
        (neighbors, neighbors_v),
        (counts, counts_v),
        (weights, weights_v),
    )
    copies = [
        pltpu.make_async_copy(source, target, local_sems.at[i])
        for i, (source, target) in enumerate(pairs)
    ]
    for copy in copies[:2]:
        copy.start()

    mesh_id = pl.DeviceIdType.MESH
    barrier = pltpu.get_barrier_semaphore()

    def signal(semaphore, k):
        pl.semaphore_signal(semaphore, inc=1, device_id=(targets[k],), device_id_type=mesh_id)

    last_line = members - far
    pl.when(me < members - 1)(lambda: signal(barrier, 0))
    signal(barrier, 1)
    pl.when(me < last_line)(lambda: signal(barrier, 2))
    pl.when(me < far)(lambda: signal(barrier, 3))
    for copy in copies[2:]:
        copy.start()

    copies[0].wait()
    copies[1].wait()
    for t in range(8):
        ghost_t[4 * t : 4 * t + 4, :] = ghost_v[:, 128 * t : 128 * t + 128]
    for k in range(4):
        index = ghost_t[pl.ds(k, 8, stride=4), :]
        lanes, rows = index & 127, index >> 7
        totals = [jnp.zeros((8, 128), FLOAT) for _ in range(3)]
        for r in range(ROWS):
            hit = rows == r
            for c in range(3):
                got = lookup(gradient_v[c : c + 1, 128 * r : 128 * r + 128], lanes)
                totals[c] = jnp.where(hit, got, totals[c])
        for c in range(3):
            outgoing[k, 8 * c : 8 * c + 8, :] = totals[c]

    for t in range(ROWS):
        gradient_t[4 * t : 4 * t + 3, :] = gradient_v[:, 128 * t : 128 * t + 128]
    for i in (2, 3, 4, 5):
        copies[i].wait()
    for t in range(ROWS):
        history_t[2 * t : 2 * t + 2, :] = history_v[:, 128 * t : 128 * t + 128]
    for b in range(BLOCKS):
        own = slice(8 * b, 8 * b + 8)
        at = slice(OWN_AT + 8 * b, OWN_AT + 8 * b + 8)
        window[0, at, :] = density_v[own, :]
        for c in range(3):
            window[1 + c, at, :] = gradient_t[pl.ds(32 * b + c, 8, stride=4), :]
        window[4, at, :] = 0.25 * size_v[own, :]
        for c in range(2):
            window[5 + c, at, :] = history_t[pl.ds(16 * b + c, 8, stride=2), :]
        window[7, at, :] = flags_v[own, :].astype(FLOAT)
    for f in range(FIELDS):
        at = MARGIN_ROWS * f
        last = OWN_AT + ROWS - MARGIN_ROWS
        edges[0, at : at + MARGIN_ROWS, :] = window[f, last : last + MARGIN_ROWS, :]
        edges[1, at : at + MARGIN_ROWS, :] = window[f, OWN_AT : OWN_AT + MARGIN_ROWS, :]

    def packet(k, target):
        return pltpu.make_async_remote_copy(
            src_ref=outgoing.at[k],
            dst_ref=incoming.at[k],
            send_sem=send_sems.at[k],
            recv_sem=recv_sems.at[k],
            device_id=(target,),
            device_id_type=mesh_id,
        )

    margins = [
        pltpu.make_async_remote_copy(
            src_ref=edges.at[k],
            dst_ref=beyond.at[k],
            send_sem=send_sems.at[4 + k],
            recv_sem=recv_sems.at[4 + k],
            device_id=(targets[k],),
            device_id_type=mesh_id,
        )
        for k in range(2)
    ]
    sends = [packet(k, targets[k]) for k in range(4)]

    heard = 3 - (me < far).astype(jnp.int32) - (me == 0).astype(jnp.int32)
    pl.semaphore_wait(barrier, heard + (me >= last_line).astype(jnp.int32))
    pl.when(me >= far)(lambda: signal(ready_sems.at[2], 3))
    pl.when(me >= last_line)(lambda: signal(ready_sems.at[3], 2))
    pl.when(me == members - 1)(lambda: signal(ready_sems.at[1], 0))
    sends[0].start()
    pl.when(me > 0)(sends[1].start)
    pl.when(me >= far)(sends[3].start)
    pl.when(me >= last_line)(sends[2].start)
    margins[0].start()
    pl.when(me > 0)(margins[1].start)

    def send_late(k, where):
        @pl.when(where)
        def _():
            pl.semaphore_wait(ready_sems.at[k], 1)
            sends[k].start()
            if k == 1:
                margins[1].start()

    start, end = me == 0, me == members - 1
    order = [
        jnp.where(start, 1, 0),
        jnp.where(start, 3, jnp.where(end, 2, 1)),
        jnp.where(start, 2, jnp.where((me < far) | end, 3, 2)),
        jnp.where(start, 0, jnp.where(end, 1, jnp.where(me < far, 2, 3))),
    ]

    def arrived(k):
        packet(k, targets[0]).wait_recv()

    copies[6].wait()
    copies[8].wait()
    for t in range(ROWS):
        index = neighbors_v[:, 128 * t : 128 * t + 128]
        neighbors_t[8 * t : 8 * t + 6, :] = index
        half = (index >> 12) & 1
        row = (index >> 7) & 31
        elsewhere = jnp.where(jnp.logical_or(index >= ELEMENTS, row >= HOT), 256, 0)
        column_t[8 * t : 8 * t + 6, :] = ((index & 127) + 128 * half + elsewhere).astype(FLOAT)
        row_t[8 * t : 8 * t + 6, :] = row
        weights_t[8 * t : 8 * t + 6, :] = weights_v[:, 128 * t : 128 * t + 128]
    for half in range(2):
        groups = [
            gradient_t[pl.ds(4 * (32 * half + 8 * q) + c, 8, stride=4), :]
            for c in range(3)
            for q in range(HOT // 8)
        ] + [jnp.zeros((8, 128), FLOAT)]
        for g in range(0, len(groups), 2):
            part = jnp.concatenate(groups[g : g + 2], axis=0)
            for s in range(3):
                piece = part.astype(jnp.bfloat16)
                at = PART * s + 8 * g
                table[at : at + 16, 128 * half : 128 * half + 128] = piece
                part = part - piece.astype(FLOAT)
    steps[...] = lax.broadcasted_iota(jnp.int32, (256, 128), 0).astype(FLOAT).astype(jnp.bfloat16)
    sublane = lax.broadcasted_iota(jnp.int32, (8, 128), 0)
    one, zero = jnp.ones((), jnp.bfloat16), jnp.zeros((), jnp.bfloat16)

    def wide(ref, at):
        return jnp.broadcast_to(ref[pl.ds(at, 1), :], (8, 128))

    def own_pairs(first, number):
        for p in range(number):
            sums = [jnp.zeros((8, 128), FLOAT) for _ in range(2)]
            rows = [2 * (first + p) + e for e in range(2)]
            for m in range(6):
                hot = []
                for e in range(2):
                    column = jnp.broadcast_to(column_t[pl.ds(8 * rows[e] + m, 1), :], (16, 128))
                    column = jnp.concatenate([column.astype(jnp.bfloat16)] * 16, axis=0)
                    hot.append(jnp.where(column == steps[...], one, zero))
                hot = jnp.concatenate(hot, axis=1)
                got = jnp.dot(table[...], hot, preferred_element_type=FLOAT)
                got = got[0 : 3 * HOT] + got[PART : PART + 3 * HOT] + got[2 * PART : 2 * PART + 3 * HOT]
                for e in range(2):
                    row = wide(row_t, 8 * rows[e] + m)
                    hits = [row == sublane + 8 * g for g in range(HOT // 8)]
                    square = None
                    for c in range(3):
                        value = jnp.zeros((8, 128), FLOAT)
                        for g in range(HOT // 8):
                            at = HOT * c + 8 * g
                            value = jnp.where(hits[g], got[at : at + 8, 128 * e : 128 * e + 128], value)
                        jump = wide(gradient_t, 4 * rows[e] + c) - value
                        square = jump * jump if square is None else square + jump * jump
                    here = jnp.logical_and((row & 7) == sublane, wide(column_t, 8 * rows[e] + m) < 256.0)
                    sums[e] = sums[e] + jnp.where(here, wide(weights_t, 8 * rows[e] + m) * square, 0.0)
            for e in range(2):
                own_sum[pl.ds(rows[e], 1), :] = jnp.sum(sums[e], axis=0, keepdims=True)

    def unit_terms(unit, group, found_rows, inside):
        block = unit // 6
        m = unit - 6 * block
        base = pl.multiple_of(block * 64, 64)
        index = neighbors_t[pl.ds(base + m, 8, stride=8), :]
        lanes, rows = index & 127, index >> 7
        totals = [jnp.zeros((8, 128), FLOAT) for _ in range(3)]
        for row, entries in found_rows:
            hit = rows == row
            for c in range(3):
                totals[c] = jnp.where(hit, lookup(entries(c), lanes), totals[c])
        square = None
        for c in range(3):
            jump = gradient_t[pl.ds(pl.multiple_of(block * 32, 32) + c, 8, stride=4), :] - totals[c]
            square = jump * jump if square is None else square + jump * jump
        weight = weights_t[pl.ds(base + m, 8, stride=8), :]
        terms[group, unit] = jnp.where(inside(rows), weight * square, 0.0)

    def rest_unit(unit):
        found_rows = [
            (r, lambda c, r=r: gradient_v[c : c + 1, 128 * r : 128 * r + 128])
            for h in range(2)
            for r in range(32 * h + HOT, 32 * h + 32)
        ]
        unit_terms(unit, 3, found_rows, lambda rows: jnp.logical_and(rows < ROWS, (rows & 31) >= HOT))

    def ghost_unit(unit, group, sources):
        found_rows = [
            (ROWS + 8 * k + s, lambda c, k=k, s=s: incoming[k, 8 * c + s : 8 * c + s + 1, :])
            for k in sources
            for s in range(8)
        ]

        def inside(rows):
            return functools.reduce(jnp.logical_or, [(rows >> 3) == 8 + k for k in sources])

        unit_terms(unit, group, found_rows, inside)

    def rest(step, carry):
        for v in range(16):
            rest_unit(16 * step + v)
        own_pairs(4 * step, 4)
        return carry

    def pair(step, carry):
        send_late(2, (step == 1) & (me < last_line))
        for v in range(16):
            ghost_unit(16 * step + v, 0, order[:2])
        own_pairs(12 + 4 * step, 4)
        return carry

    lax.fori_loop(0, 3, rest, 0)
    arrived(order[0])
    arrived(order[1])
    lax.fori_loop(0, 3, pair, 0)
    send_late(3, me < far)
    arrived(order[2])
    for v in range(48):
        ghost_unit(v, 1, order[2:3])
    own_pairs(24, 4)
    send_late(1, start)
    arrived(order[3])
    for v in range(48):
        ghost_unit(v, 2, order[3:])
    own_pairs(28, 4)
    for margin in margins:
        margin.wait_recv()
    for f in range(FIELDS):
        at = MARGIN_ROWS * f
        window[f, OWN_AT - MARGIN_ROWS : OWN_AT, :] = beyond[0, at : at + MARGIN_ROWS, :]
        right = OWN_AT + ROWS
        window[f, right : right + 8, :] = jnp.zeros((8, 128), FLOAT)
        window[f, right + 8 : right + 16, :] = jnp.zeros((8, 128), FLOAT)
        window[f, right : right + MARGIN_ROWS, :] = beyond[1, at : at + MARGIN_ROWS, :]
    copies[7].wait()
    counts_out[...] = counts_v[...]
    for send in sends + margins:
        send.wait_send()


def finish(members, window, own_sum, terms, counts, indicator, children, shifted, indicator_v, children_v, sems):
    me = lax.axis_index("dom")
    owners = lax.broadcasted_iota(jnp.int32, (1, 128), 1)
    held = counts[...]
    begin = jnp.sum(jnp.where(owners < me, held, 0))
    count = jnp.sum(jnp.where(owners == me, held, 0))
    count = jnp.minimum(count, members * ELEMENTS - begin)
    start = jnp.clip(begin - me * ELEMENTS + MARGIN, 0, 2 * MARGIN)
    first, turn = start // 128, start % 128
    first = first + OWN_AT - MARGIN_ROWS
    lane = lax.broadcasted_iota(jnp.int32, (8, 128), 1)
    slot = lax.broadcasted_iota(jnp.int32, (8, 128), 0) * 128 + lane
    turned = (lane + turn) & 127
    low = lane < 128 - turn

    def shift(b):
        for f in range(FIELDS):
            here = window[f, pl.ds(first + 8 * b, 8), :]
            there = window[f, pl.ds(first + 8 * b + 1, 8), :]
            both = [jnp.take_along_axis(v, turned, axis=1, mode="promise_in_bounds") for v in (here, there)]
            value = jnp.where(low, both[0], both[1])
            if f in (0, 5, 6, 7):
                value = jnp.where(slot + 1024 * b < count, value, 0.0)
            shifted[f, 8 * b : 8 * b + 8, :] = value

    child = lax.broadcasted_iota(jnp.int32, (8, 128), 0)
    signs = [(2 * ((child >> c) & 1) - 1).astype(FLOAT) for c in range(3)]
    eldest = child == 0
    copies = []
    for t in range(OUT_ROWS):
        if t % CHUNK == 0:
            for b in range(t // 8, (t + CHUNK) // 8):
                shift(b)
        row = [jnp.broadcast_to(shifted[f, t : t + 1, :], (8, 128)) for f in range(FIELDS)]
        slope = signs[0] * row[1] + signs[1] * row[2] + signs[2] * row[3]
        refined = row[7] > 0.0
        kept = jnp.logical_or(refined, eldest)
        at = slice(128 * t, 128 * t + 128)
        moved = jnp.where(refined, row[0] + row[4] * slope, row[0])
        children_v[0, :, at] = jnp.where(kept, moved, 0.0)
        children_v[1, :, at] = jnp.where(kept, row[5], 0.0)
        children_v[2, :, at] = jnp.where(kept, row[6], 0.0)
        if (t + 1) % CHUNK == 0:
            part = pl.ds(128 * (t + 1 - CHUNK), 128 * CHUNK)
            out = pltpu.make_async_copy(children_v.at[:, :, part], children.at[:, :, part], sems.at[t // CHUNK])
            out.start()
            copies.append(out)
    for block in range(BLOCKS):
        total = own_sum[8 * block : 8 * block + 8, :]
        for m in range(6):
            for group in range(4):
                total = total + terms[group, 6 * block + m]
        indicator_v[8 * block : 8 * block + 8, :] = total
    out = pltpu.make_async_copy(indicator_v, indicator, sems.at[OUT_ROWS // CHUNK])
    out.start()
    for copy in copies + [out]:
        copy.wait()


def local(
    members,
    density,
    gradient,
    elem_size,
    history,
    refine_flags,
    face_neighbor,
    face_weight,
    ghost_send,
    new_counts,
):
    vmem = pltpu.VMEM
    flat = (ROWS, 128)
    operands = (
        density.reshape(flat),
        gradient,
        elem_size.reshape(flat),
        history,
        refine_flags.reshape(flat),
        face_neighbor,
        face_weight,
        ghost_send,
        new_counts.reshape(1, 128),
    )
    operands = [pltpu.with_memory_space_constraint(x, pltpu.HBM) for x in operands]
    handed = pl.pallas_call(
        functools.partial(kernel, members),
        out_shape=(
            vmem((FIELDS, WINDOW, 128), FLOAT),
            vmem(flat, FLOAT),
            vmem((4, 6 * BLOCKS, 8, 128), FLOAT),
            vmem((1, 128), jnp.int32),
        ),
        in_specs=[pl.BlockSpec(memory_space=pltpu.HBM)] * 9,
        out_specs=(pl.BlockSpec(memory_space=vmem),) * 4,
        scratch_shapes=[
            vmem(flat, FLOAT),
            vmem((3, ELEMENTS), FLOAT),
            vmem(flat, FLOAT),
            vmem((2, ELEMENTS), FLOAT),
            vmem(flat, jnp.int32),
            vmem((6, ELEMENTS), jnp.int32),
            vmem((6, ELEMENTS), FLOAT),
            vmem((4, GHOST), jnp.int32),
            vmem((1, 128), jnp.int32),
            vmem((4 * ROWS, 128), FLOAT),
            vmem((2 * ROWS, 128), FLOAT),
            vmem((8 * ROWS, 128), jnp.int32),
            vmem((8 * ROWS, 128), FLOAT),
            vmem((32, 128), jnp.int32),
            vmem((8 * ROWS, 128), FLOAT),
            vmem((8 * ROWS, 128), jnp.int32),
            vmem((3 * PART, 256), jnp.bfloat16),
            vmem((256, 128), jnp.bfloat16),
            vmem((4, 24, 128), FLOAT),
            vmem((4, 24, 128), FLOAT),
            vmem((2, FIELDS * MARGIN_ROWS, 128), FLOAT),
            vmem((2, FIELDS * MARGIN_ROWS, 128), FLOAT),
            pltpu.SemaphoreType.DMA((9,)),
            pltpu.SemaphoreType.DMA((6,)),
            pltpu.SemaphoreType.DMA((6,)),
            pltpu.SemaphoreType.REGULAR((4,)),
        ],
        compiler_params=pltpu.CompilerParams(
            collective_id=0, has_side_effects=True, vmem_limit_bytes=32 * 1024 * 1024
        ),
    )(*operands)
    handed = [pltpu.with_memory_space_constraint(x, vmem) for x in handed]
    indicator, children = pl.pallas_call(
        functools.partial(finish, members),
        out_shape=(pltpu.HBM(flat, FLOAT), pltpu.HBM((3, 8, CAPACITY), FLOAT)),
        in_specs=[pl.BlockSpec(memory_space=vmem)] * 4,
        out_specs=(pl.BlockSpec(memory_space=pltpu.HBM),) * 2,
        scratch_shapes=[
            vmem((FIELDS, OUT_ROWS, 128), FLOAT),
            vmem(flat, FLOAT),
            vmem((3, 8, CAPACITY), FLOAT),
            pltpu.SemaphoreType.DMA((OUT_ROWS // CHUNK + 1,)),
        ],
        compiler_params=pltpu.CompilerParams(vmem_limit_bytes=8 * 1024 * 1024),
    )(*handed)
    return indicator.reshape(ELEMENTS), children


def solution(mesh):
    placed = (
        P("dom"),
        P(None, "dom"),
        P("dom"),
        P(None, "dom"),
        P("dom"),
        P(None, "dom"),
        P(None, "dom"),
        P("dom", None),
        P(),
    )
    return jax.shard_map(
        functools.partial(local, mesh.shape["dom"]),
        mesh=mesh,
        in_specs=placed,
        out_specs=(P("dom"), P(None, None, "dom")),
        check_vma=False,
    )
```
